768 devices in a mesh: row: 192 (over x, z, y_hi, core), col: 4 (over y_lo).
Axes of the slice: x: 4, y: 8 (y_hi: 2, y_lo: 4; y = y_hi * 4 + y_lo), z: 12, core: 2. Of those that a mesh axis runs over, the one named last changes fastest.
Arguments:
- out_grad: bfloat16 [1536, 8192], P('row', 'col'), may hold values from -6 to 6
- down_weight: bfloat16 [24576, 8192], P('row', 'col'), may hold values from -0.0546875 to 0.0546875
- block_mask: int32 [192, 64], P('row', 'col'), may hold values from 0 to 1, as said below
- gate_act: bfloat16 [1536, 24576], P('col', 'row'), may hold values from -6 to 6
- up_act: bfloat16 [1536, 24576], P('col', 'row'), may hold values from -6 to 6
Outputs:
- grad_gate: bfloat16 [1536, 24576], P('col', 'row')
- grad_up: bfloat16 [1536, 24576], P('col', 'row')
- grad_down: bfloat16 [24576, 8192], P('row', 'col')
The draws below stay inside these ranges and needn't reach their ends.
Inputs may be any that keep to these rules, and one draw needn't show every extreme that they name: `block_mask`: in each block row, every aligned group of 16 blocks along the features holds between 4 and 12 ones, and some group holds exactly 12.
All inputs are finite; a program needn't handle non-finite values.
Results may differ from the reference program's by a relative error of at most 0.0049.
Values may be sent and summed in bfloat16 or wider, within the bound.
A program may use at most 32 MiB of HBM per device.

```python
import jax
import jax.numpy as jnp
from jax import lax

D = 8192
FF = 24576
BLK = 128
TOKENS = 1536
NBD = 16
MAXNZ = 12


def draw_block_mask(key, part):
    key = jax.random.fold_in(key, 7)
    key_count, key_score, key_pick = jax.random.split(key, 3)
    block_rows = FF // BLK
    groups = D // (BLK * NBD)
    lowest = max(1, MAXNZ // 3)
    counts = jax.random.randint(key_count, (block_rows, groups), lowest, MAXNZ + 1)
    chosen = jax.random.randint(key_pick, (), 0, block_rows * groups)
    flat_ids = jnp.arange(block_rows * groups, dtype=jnp.int32).reshape(block_rows, groups)
    counts = jnp.where(flat_ids == chosen, MAXNZ, counts)
    scores = jax.random.randint(key_score, (block_rows, groups, NBD), 0, 2 ** 20) * NBD
    scores = scores + jnp.arange(NBD, dtype=jnp.int32)
    ranks = jnp.argsort(jnp.argsort(scores, axis=2), axis=2)
    kept = (ranks < counts[:, :, None]).astype(jnp.int32)
    return kept.reshape(block_rows, groups * NBD)


def block_scale(rng, shape, cuts, least, largest):
    loudness = 1.0
    for dim, blocks in cuts:
        draws = jax.random.uniform(jax.random.fold_in(jax.random.fold_in(rng, 6), dim), (blocks,), jnp.float32, least / len(cuts), largest / len(cuts))
        loudness = loudness * jnp.repeat(jnp.exp(draws), shape[dim] // blocks).reshape((-1,) + (1,) * (len(shape) - 1 - dim))
    return loudness


def bell_draw(rng, dims, scale, bound, shards=(), kind=jnp.bfloat16):
    level = block_scale(rng, dims, shards, -0.22, 0.18) if shards else 1.0
    drawn = jax.random.normal(rng, dims, jnp.float32) * scale * level
    return jnp.minimum(jnp.maximum(drawn, -bound), bound).astype(kind)


def setup_inputs(seed: int = 0) -> dict:
    key_list = jax.random.split(jax.random.key(seed), 6)
    return {
        "out_grad": bell_draw(key_list[0], (TOKENS, D), 1.0, 6.0, ((0, 192), (1, 4))),
        "down_weight": bell_draw(key_list[1], (FF, D), (FF // 2) ** -0.5, 0.0546875, ((0, 192), (1, 4))),
        "block_mask": draw_block_mask(jax.random.fold_in(key_list[5], 71), 0),
        "gate_act": bell_draw(key_list[3], (TOKENS, FF), 1.5, 6.0, ((0, 4), (1, 192))),
        "up_act": bell_draw(key_list[4], (TOKENS, FF), 1.0, 6.0, ((0, 4), (1, 192))),
    }


def reference(out_grad, down_weight, block_mask, gate_act, up_act):
    expand = jnp.repeat(jnp.repeat(block_mask.astype(jnp.bfloat16), BLK, 0), BLK, 1)
    kept = down_weight * expand
    gate_f = gate_act.astype(jnp.float32)
    up_f = up_act.astype(jnp.float32)
    sig = jax.nn.sigmoid(gate_f)
    hidden = (gate_f * sig * up_f).astype(jnp.bfloat16)
    grad_hidden = lax.dot_general(out_grad, kept, (((1,), (1,)), ((), ())), preferred_element_type=jnp.float32)
    grad_up = (grad_hidden * gate_f * sig).astype(jnp.bfloat16)
    grad_gate = (grad_hidden * up_f * sig * (1.0 + gate_f * (1.0 - sig))).astype(jnp.bfloat16)
    grad_down = lax.dot_general(hidden, out_grad, (((0,), (0,)), ((), ())), preferred_element_type=jnp.float32)
    grad_down = (grad_down * expand.astype(jnp.float32)).astype(jnp.bfloat16)
    return grad_gate, grad_up, grad_down
```

```python
import jax
import jax.numpy as jnp
from jax import lax
from jax.experimental import pallas as pl
from jax.experimental.pallas import tpu as pltpu
from jax.sharding import PartitionSpec as P

MESH = pl.DeviceIdType.MESH
F32 = jnp.float32
BF16 = jnp.bfloat16

BLK = 128
NX, NZ, NH, NC, NCOL = 4, 12, 2, 2, 4
HALF = 1024
FA = 384
FB = HALF - FA
ROWS = 32
STEPS = NZ // 2
GROUPS = STEPS + 1


def slots(g):
    if g == 0:
        return 0, 1
    if g == STEPS:
        return NZ - 1, NZ
    return 2 * g - 1, 2 * g + 1


def slot_offset(r):
    if r == 0:
        return 0
    if r == NZ - 1:
        return STEPS
    s = (r + 1) // 2
    return -s if r % 2 else s


def kernel(
    x_ref, w_ref, mask_ref, gate_ref, up_ref,
    gg_ref, gu_ref, gd_ref,
    pack, quart, ga, gb, wm, hs, acc, tbuf, pbuf, rbuf,
    init_s, init_r, ax_s, ax_r, az_s, az_r, bz_s, bz_r, bx_s, bx_r,
    sa_s, sa_r, sb_s, sb_r, h_s, h_r, p_s, p_r,
):
    row, col = lax.axis_index("row"), lax.axis_index("col")
    c = lax.rem(row, NC)
    h = lax.rem(row // NC, NH)
    z0 = lax.rem(row // (NC * NH), NZ)
    x0 = row // (NC * NH * NZ)
    d = 1 - 2 * c

    def device(x, z, hh, cc):
        return (((x * NZ + z) * NH + hh) * NC + cc, col)

    xf = device(lax.rem(x0 + d + NX, NX), z0, h, c)
    xb = device(lax.rem(x0 - d + NX, NX), z0, h, c)
    zf = device(x0, lax.rem(z0 + d + NZ, NZ), h, c)
    zb = device(x0, lax.rem(z0 - d + NZ, NZ), h, c)
    sib = device(x0, z0, h, 1 - c)
    far0 = device(x0, z0, 1 - h, c)
    far1 = device(x0, z0, 1 - h, 1 - c)
    cols = [(row, lax.rem(col + k, NCOL)) for k in range(1, NCOL)]

    def copy(src, dst, send, recv, to):
        return pltpu.make_async_remote_copy(
            src_ref=src, dst_ref=dst, send_sem=send, recv_sem=recv,
            device_id=to, device_id_type=MESH,
        )

    sent = []

    def start(cp):
        cp.start()
        sent.append(cp)

    barrier = pltpu.get_barrier_semaphore()
    peers = [sib, far0, far1, xf, xb, zf, zb] + cols
    for peer in peers:
        pl.semaphore_signal(barrier, inc=1, device_id=peer, device_id_type=MESH)

    xs = x_ref[...].astype(F32)
    q = HALF // 2
    for cc in range(NC):
        pack[cc] = jnp.concatenate(
            [xs[:, cc * HALF:cc * HALF + q], xs[:, cc * HALF + q:(cc + 1) * HALF]], axis=0
        ).astype(BF16)
    pl.semaphore_wait(barrier, len(peers))

    first = [
        copy(pack.at[1 - c], quart.at[h, c], init_s.at[0], init_r.at[0], sib),
        copy(pack.at[c], quart.at[h, c], init_s.at[1], init_r.at[1], far0),
        copy(pack.at[1 - c], quart.at[h, c], init_s.at[2], init_r.at[2], far1),
    ]
    for cp in first:
        start(cp)

    quart[h, c] = pack[c]
    for b in range(2 * HALF // BLK):
        lanes = slice(b * BLK, (b + 1) * BLK)
        wm[:, lanes] = (w_ref[:, lanes].astype(F32) * mask_ref[0, b].astype(F32)).astype(BF16)
    places = []
    for r in range(NZ):
        z = lax.rem(z0 + slot_offset(r) + NZ, NZ)
        places.append(pl.ds(pl.multiple_of(z * ROWS, ROWS), ROWS))
    for r in range(NZ):
        gate = gate_ref[places[r], :].astype(F32)
        up = up_ref[places[r], :].astype(F32)
        hs[col, r] = (gate * jax.nn.sigmoid(gate) * up).astype(BF16)

    for cp in first:
        cp.wait_recv()
    for hh in range(NH):
        parts = []
        for cc in range(NC):
            v = quart[hh, cc].astype(F32)
            parts.append(jnp.concatenate([v[0:8], v[8:16]], axis=1))
        block = jnp.concatenate(parts, axis=0).astype(BF16)
        ga[c, x0, 0, 16 * hh:16 * hh + 16, :] = block[:, :FA]
        gb[c, x0, 0, 16 * hh:16 * hh + 16, :] = block[:, FA:]

    def zslot(way, s):
        if s == 0:
            return 0
        if s == STEPS:
            return NZ - 1
        return 2 * s - 1 + c if way == 0 else 2 * s - c

    ways = [(zf, STEPS), (zb, STEPS - 1)]

    def bz(way, s):
        src, dst = zslot(way, s - 1), zslot(way, s)
        i = way * STEPS + s - 1
        return copy(gb.at[c, x0, src], gb.at[c, x0, dst], bz_s.at[i], bz_r.at[i], ways[way][0])

    def az(way, s):
        src, dst = zslot(way, s - 1), zslot(way, s)
        i = way * STEPS + s - 1
        return copy(ga.at[c, :, src], ga.at[c, :, dst], az_s.at[i], az_r.at[i], ways[way][0])

    xprev = lax.rem(x0 - d + NX, NX)

    def ax(k):
        xs_ = xprev if k == 1 else x0
        ref = ga.at[c, xs_, 0]
        return copy(ref, ref, ax_s.at[k], ax_r.at[k], xb if k == 2 else xf)

    def bx(g, k):
        lo, hi = slots(g)
        xs_ = xprev if k == 1 else x0
        ref = gb.at[c, xs_, pl.ds(lo, hi - lo)]
        return copy(ref, ref, bx_s.at[g, k], bx_r.at[g, k], xb if k == 2 else xf)

    def sa(g):
        lo, hi = slots(g)
        ref = ga.at[c, :, pl.ds(lo, hi - lo)]
        return copy(ref, ref, sa_s.at[g], sa_r.at[g], sib)

    def sb(g):
        lo, hi = slots(g)
        ref = gb.at[c, :, pl.ds(lo, hi - lo)]
        return copy(ref, ref, sb_s.at[g], sb_r.at[g], sib)

    def hid(k):
        ref = hs.at[col]
        return copy(ref, ref, h_s.at[k], h_r.at[k], cols[k])

    def part(g, k):
        lo, hi = slots(g)
        dest = lax.rem(col + k + 1, NCOL)
        return copy(
            pbuf.at[dest, pl.ds(lo, hi - lo)], rbuf.at[k, pl.ds(lo, hi - lo)],
            p_s.at[g, k], p_r.at[g, k], cols[k],
        )

    def compute(g):
        sa(g).wait_recv()
        sb(g).wait_recv()
        lo, hi = slots(g)
        tokens = NX * (hi - lo) * ROWS
        hid_g = hs[:, lo:hi].reshape(tokens, BLK)
        term = None
        for cc in range(NC):
            for buf, at, n in ((ga, 0, FA), (gb, FA, FB)):
                v = buf[cc, :, lo:hi].reshape(tokens, n)
                lanes = slice(cc * HALF + at, cc * HALF + at + n)
                t = lax.dot_general(
                    v, wm[:, lanes], (((1,), (1,)), ((), ())), preferred_element_type=F32
                )
                term = t if term is None else term + t
        term = term.reshape(NX, hi - lo, ROWS, BLK)
        tbuf[:, lo:hi] = term
        pbuf[:, lo:hi] = term.astype(BF16)
        for k in range(NCOL - 1):
            start(part(g, k))
        for cc in range(NC):
            for buf, at, n in ((ga, 0, FA), (gb, FA, FB)):
                v = buf[cc, :, lo:hi].reshape(tokens, n)
                lanes = slice(cc * HALF + at, cc * HALF + at + n)
                t = lax.dot_general(
                    hid_g, v, (((0,), (0,)), ((), ())), preferred_element_type=F32
                )
                acc[:, lanes] = t if g == 0 else acc[:, lanes] + t

    for way in range(2):
        start(bz(way, 1))
    start(ax(0))
    start(ax(2))
    start(bx(0, 0))
    start(bx(0, 2))
    for k in range(NCOL - 1):
        start(hid(k))
    ax(0).wait_recv()
    start(ax(1))
    ax(2).wait_recv()
    ax(1).wait_recv()
    for way in range(2):
        start(az(way, 1))
    start(sa(0))

    for s in range(1, STEPS + 1):
        for way in range(2):
            if s <= ways[way][1]:
                bz(way, s).wait_recv()
                if s < ways[way][1]:
                    start(bz(way, s + 1))
        start(bx(s, 0))
        start(bx(s, 2))
        bx(s - 1, 0).wait_recv()
        start(bx(s - 1, 1))
        for way in range(2):
            if s <= ways[way][1]:
                az(way, s).wait_recv()
                if s < ways[way][1]:
                    start(az(way, s + 1))
        start(sa(s))
        bx(s - 1, 2).wait_recv()
        bx(s - 1, 1).wait_recv()
        start(sb(s - 1))
        if s == 2:
            for k in range(NCOL - 1):
                hid(k).wait_recv()
        if s >= 2:
            compute(s - 2)
    last = STEPS
    bx(last, 0).wait_recv()
    start(bx(last, 1))
    compute(last - 1)
    bx(last, 2).wait_recv()
    bx(last, 1).wait_recv()
    start(sb(last))
    compute(last)

    for b in range(2 * HALF // BLK):
        lanes = slice(b * BLK, (b + 1) * BLK)
        gd_ref[:, lanes] = (acc[:, lanes] * mask_ref[0, b].astype(F32)).astype(BF16)
    for g in range(GROUPS):
        for k in range(NCOL - 1):
            part(g, k).wait_recv()
    for r in range(NZ):
        gate = gate_ref[places[r], :].astype(F32)
        up = up_ref[places[r], :].astype(F32)
        sig = jax.nn.sigmoid(gate)
        gh = tbuf[col, r]
        for k in range(NCOL - 1):
            gh = gh + rbuf[k, r].astype(F32)
        gu_ref[places[r], :] = (gh * gate * sig).astype(BF16)
        gg_ref[places[r], :] = (gh * up * sig * (1.0 + gate * (1.0 - sig))).astype(BF16)
    for cp in sent:
        cp.wait_send()


def shards(out_grad, down_weight, block_mask, gate_act, up_act):
    vmem = pl.BlockSpec(memory_space=pltpu.VMEM)
    smem = pl.BlockSpec(memory_space=pltpu.SMEM)
    dma = pltpu.SemaphoreType.DMA
    units = down_weight.shape[0]
    rings = 2 * STEPS - 1
    scratch = [
        pltpu.VMEM((NC, 16, HALF // 2), BF16),
        pltpu.VMEM((NH, NC, 16, HALF // 2), BF16),
        pltpu.VMEM((NC, NX, NZ, ROWS, FA), BF16),
        pltpu.VMEM((NC, NX, NZ, ROWS, FB), BF16),
        pltpu.VMEM((units, NC * HALF), BF16),
        pltpu.VMEM((NX, NZ, ROWS, units), BF16),
        pltpu.VMEM((units, NC * HALF), F32),
        pltpu.VMEM((NX, NZ, ROWS, units), F32),
        pltpu.VMEM((NX, NZ, ROWS, units), BF16),
        pltpu.VMEM((NCOL - 1, NZ, ROWS, units), BF16),
    ]
    for shape in ((3,), (3,), (rings,), (rings,), (GROUPS, 3), (GROUPS,), (GROUPS,), (NCOL - 1,), (GROUPS, NCOL - 1)):
        scratch += [dma(shape), dma(shape)]
    return pl.pallas_call(
        kernel,
        out_shape=(
            jax.ShapeDtypeStruct(gate_act.shape, BF16),
            jax.ShapeDtypeStruct(up_act.shape, BF16),
            jax.ShapeDtypeStruct(down_weight.shape, BF16),
        ),
        in_specs=[vmem, vmem, smem, vmem, vmem],
        out_specs=(vmem, vmem, vmem),
        scratch_shapes=scratch,
        compiler_params=pltpu.CompilerParams(
            collective_id=0, has_side_effects=True, vmem_limit_bytes=40 * 1024 * 1024
        ),
    )(out_grad, down_weight, block_mask, gate_act, up_act)


def solution(mesh):
    in_specs = (P("row", "col"), P("row", "col"), P("row", "col"), P("col", "row"), P("col", "row"))
    out_specs = (P("col", "row"), P("col", "row"), P("row", "col"))
    return jax.shard_map(shards, mesh=mesh, in_specs=in_specs, out_specs=out_specs, check_vma=False)
```

```python
import heapq

import jax
import jax.numpy as jnp
from jax import lax
from jax.experimental import pallas as pl
from jax.experimental.pallas import tpu as pltpu
from jax.sharding import PartitionSpec as P

MESH = pl.DeviceIdType.MESH
F32 = jnp.float32
BF16 = jnp.bfloat16

BLK = 128
NX, NZ, NH, NC, NCOL = 4, 12, 2, 2, 4
TOK = 8
PACK = 2 * TOK
HALF = 1024
ROWS = NH * NC * TOK
STEPS = NZ // 2
GROUPS = STEPS + 1
WAYS = (STEPS, STEPS - 1)

STREAMS = (
    (0, "zx", 384, 640),
    (0, "xz", 0, 384),
    (1, "zx", 384, 640),
    (1, "xz", 0, 384),
)


def slots(g):
    if g == 0:
        return 0, 1
    if g == STEPS:
        return NZ - 1, NZ
    return 2 * g - 1, 2 * g + 1


def slot_offset(r):
    if r == 0:
        return 0
    if r == NZ - 1:
        return STEPS
    s = (r + 1) // 2
    return -s if r % 2 else s


def make_plan():
    rate = {"z": 91e3, "x": 91e3, "sib": 400e3}
    free = {"z": 0.0, "x": 0.0, "sib": 0.0}
    latency, issue = 0.9, 0.06
    ops, arrivals = [], []
    now = 0.0
    seen = {}
    ready = [0] * GROUPS
    todo = []

    def start(msg, kind, size):
        nonlocal now
        ops.append(("start", msg))
        now += issue
        free[kind] = max(free[kind], now) + size / rate[kind]
        heapq.heappush(arrivals, (free[kind] + latency, msg))

    def size(i, slots_, xs):
        return slots_ * xs * PACK * STREAMS[i][3] * 2

    def nslots(g):
        lo, hi = slots(g)
        return hi - lo

    def send_z(i, way, s):
        start(("z", i, way, s), "z", size(i, 1, 1 if STREAMS[i][1] == "zx" else NX))

    def send_x(i, g, k):
        start(("x", i, g, k), "x", size(i, nslots(g), 1))

    def send_sib(i, g):
        start(("sib", i, g), "sib", size(i, nslots(g), NX))

    def begin(i):
        if STREAMS[i][1] == "zx":
            send_z(i, 0, 1)
            send_z(i, 1, 1)
        send_x(i, 0, 0)
        send_x(i, 0, 2)

    def count(key, full):
        seen[key] = seen.get(key, 0) + 1
        return seen[key] == full

    for i in (0, 1):
        begin(i)
    ops.append(("prepare",))
    now += 1.5
    heapq.heappush(arrivals, (5.5, ("far",)))
    heapq.heappush(arrivals, (9.0, ("hid",)))
    done = 0
    while arrivals or todo:
        if todo and (not arrivals or arrivals[0][0] > now):
            g = todo.pop(0)
            ops.append(("compute", g))
            now += 0.6 if g in (0, STEPS) else 1.0
            continue
        at, msg = heapq.heappop(arrivals)
        now = max(now, at) + issue
        if msg[0] == "sib":
            ready[msg[2]] += 1
            while done < GROUPS and ready[done] == len(STREAMS) and seen.get("hid"):
                todo.append(done)
                done += 1
            continue
        ops.append(("wait", msg))
        if msg[0] == "far":
            for i in (2, 3):
                begin(i)
        elif msg[0] == "hid":
            seen["hid"] = 1
        elif msg[0] == "z":
            _, i, way, s = msg
            if s < WAYS[way]:
                send_z(i, way, s + 1)
            if count(("z", i, s), 1 if s == STEPS else 2):
                if STREAMS[i][1] == "zx":
                    send_x(i, s, 0)
                    send_x(i, s, 2)
                else:
                    send_sib(i, s)
        else:
            _, i, g, k = msg
            if k == 0:
                send_x(i, g, 1)
            if count(("x", i, g), 3):
                if STREAMS[i][1] == "xz":
                    send_z(i, 0, 1)
                    send_z(i, 1, 1)
                send_sib(i, g)
    return ops, now


def kernel(
    x_hbm, w_hbm, mask_hbm, gate_hbm, up_hbm,
    gg_ref, gu_ref, gd_ref,
    xv, wv, mask, gv, uv, data, wm, hs, acc, tbuf, pbuf, rbuf,
    in_s, far_s, far_r, z_s, z_r, x_s, x_r, sib_s, sib_r, h_s, h_r, p_s, p_r,
):
    row, col = lax.axis_index("row"), lax.axis_index("col")
    c = lax.rem(row, NC)
    h = lax.rem(row // NC, NH)
    z0 = lax.rem(row // (NC * NH), NZ)
    x0 = row // (NC * NH * NZ)
    d = 1 - 2 * c
    xprev = lax.rem(x0 - d + NX, NX)

    def device(x, z, hh, cc):
        return (((x * NZ + z) * NH + hh) * NC + cc, col)

    xf = device(lax.rem(x0 + d + NX, NX), z0, h, c)
    xb = device(xprev, z0, h, c)
    zw = (device(x0, lax.rem(z0 + d + NZ, NZ), h, c), device(x0, lax.rem(z0 - d + NZ, NZ), h, c))
    sib = device(x0, z0, h, 1 - c)
    far = device(x0, z0, 1 - h, c)
    cols = [(row, lax.rem(col + k, NCOL)) for k in range(1, NCOL)]

    def copy(src, dst, send, recv, to):
        return pltpu.make_async_remote_copy(
            src_ref=src, dst_ref=dst, send_sem=send, recv_sem=recv,
            device_id=to, device_id_type=MESH,
        )

    barrier = pltpu.get_barrier_semaphore()
    peers = [xf, xb, *zw, sib, far] + cols
    loads = [
        pltpu.make_async_copy(src, dst, in_s.at[k])
        for k, (src, dst) in enumerate(
            ((x_hbm, xv), (w_hbm, wv), (mask_hbm, mask), (gate_hbm, gv), (up_hbm, uv))
        )
    ]
    loads[0].start()
    for peer in peers:
        pl.semaphore_signal(barrier, inc=1, device_id=peer, device_id_type=MESH)
    for load in loads[1:]:
        load.start()
    loads[0].wait()
    xs = xv[...].astype(F32)
    data[c, x0, 0, h] = jnp.concatenate([xs[:, :HALF], xs[:, HALF:]], axis=0).astype(BF16)
    pl.semaphore_wait(barrier, len(peers))

    def zslot(way, s):
        if s == 0:
            return 0
        if s == STEPS:
            return NZ - 1
        return 2 * s - 1 + c if way == 0 else 2 * s - c

    def cut(i, core, xsel, rsel):
        whose, _, lane, n = STREAMS[i]
        return data.at[core, xsel, rsel, h if whose == 0 else 1 - h, :, pl.ds(lane, n)]

    def span(g):
        lo, hi = slots(g)
        return pl.ds(lo, hi - lo)

    def describe(msg):
        kind = msg[0]
        if kind == "far":
            ref = data.at[c, x0, 0, h]
            return copy(ref, ref, far_s, far_r, far)
        if kind == "hid":
            ref = hs.at[col]
            return copy(ref, ref, h_s, h_r.at[msg[1]], cols[msg[1]])
        if kind == "part":
            _, g, k = msg
            src = pbuf.at[lax.rem(col + k + 1, NCOL), span(g)]
            return copy(src, rbuf.at[k, span(g)], p_s, p_r, cols[k])
        if kind == "z":
            _, i, way, s = msg
            xsel = x0 if STREAMS[i][1] == "zx" else slice(None)
            src, dst = cut(i, c, xsel, zslot(way, s - 1)), cut(i, c, xsel, zslot(way, s))
            return copy(src, dst, z_s.at[i], z_r.at[i, way * STEPS + s - 1], zw[way])
        if kind == "x":
            _, i, g, k = msg
            ref = cut(i, c, xprev if k == 1 else x0, span(g))
            return copy(ref, ref, x_s.at[i], x_r.at[i, 3 * g + k], xb if k == 2 else xf)
        _, i, g = msg
        ref = cut(i, c, slice(None), span(g))
        return copy(ref, ref, sib_s, sib_r.at[g], sib)

    def compute(g):
        ref = data.at[1 - c, :, span(g)]
        copy(ref, ref, sib_s, sib_r.at[g], sib).wait_recv()
        lo, hi = slots(g)
        nr = hi - lo
        tokens = NX * nr * NH * PACK
        hid = hs[:, lo:hi].astype(F32).reshape(NX, nr, NH, NC, TOK, BLK)
        blocks = [data[cc, :, lo:hi].reshape(tokens, HALF) for cc in range(NC)]
        terms, hids = [], []
        for cc in range(NC):
            t = lax.dot_general(
                blocks[cc], wm[...], (((1,), (1,)), ((), ())), preferred_element_type=F32
            ).reshape(NX, nr, NH, 2, TOK, 2 * BLK)
            terms.append(t[:, :, :, 0, :, :BLK] + t[:, :, :, 1, :, BLK:])
            v = hid[:, :, :, cc]
            zero = jnp.zeros_like(v)
            both = jnp.concatenate(
                [jnp.concatenate([v, zero], axis=-1), jnp.concatenate([zero, v], axis=-1)], axis=-2
            )
            hids.append(both.reshape(tokens, 2 * BLK).astype(BF16))
        term = jnp.concatenate(terms, axis=-2).reshape(NX, nr, ROWS, BLK)
        tbuf[:, lo:hi] = term
        pbuf[:, lo:hi] = term.astype(BF16)
        for k in range(NCOL - 1):
            describe(("part", g, k)).start()
        t = lax.dot_general(
            jnp.concatenate(hids, axis=0), jnp.concatenate(blocks, axis=0),
            (((0,), (0,)), ((), ())), preferred_element_type=F32,
        )
        acc[...] = t if g == 0 else acc[...] + t

    places = []
    for r in range(NZ):
        z = lax.rem(z0 + slot_offset(r) + NZ, NZ)
        places.append(pl.ds(pl.multiple_of(z * ROWS, ROWS), ROWS))

    def prepare():
        loads[3].wait()
        loads[4].wait()
        for r in range(NZ):
            gate = gv[places[r], :].astype(F32)
            up = uv[places[r], :].astype(F32)
            hs[col, r] = (gate * jax.nn.sigmoid(gate) * up).astype(BF16)
        for k in range(NCOL - 1):
            describe(("hid", k)).start()
        loads[1].wait()
        loads[2].wait()
        for b in range(2 * HALF // BLK):
            part, at = divmod(b * BLK, HALF)
            scale = mask[0, b].astype(F32)
            value = wv[:, b * BLK:(b + 1) * BLK].astype(F32) * scale
            wm[part * BLK:(part + 1) * BLK, at:at + BLK] = value.astype(BF16)

    describe(("far",)).start()
    for op in make_plan()[0]:
        if op[0] == "prepare":
            prepare()
        elif op[0] == "compute":
            compute(op[1])
        elif op[0] == "start":
            describe(op[1]).start()
        elif op[1][0] == "hid":
            for k in range(NCOL - 1):
                describe(("hid", k)).wait_recv()
        else:
            describe(op[1]).wait_recv()

    for b in range(2 * HALF // BLK):
        part, at = divmod(b * BLK, HALF)
        scale = mask[0, b].astype(F32)
        value = acc[part * BLK:(part + 1) * BLK, at:at + BLK] * scale
        gd_ref[:, b * BLK:(b + 1) * BLK] = value.astype(BF16)
    copy(rbuf, rbuf, p_s, p_r, sib).wait_recv()
    for r in range(NZ):
        gate = gv[places[r], :].astype(F32)
        up = uv[places[r], :].astype(F32)
        sig = jax.nn.sigmoid(gate)
        gh = tbuf[col, r]
        for k in range(NCOL - 1):
            gh = gh + rbuf[k, r].astype(F32)
        gu_ref[places[r], :] = (gh * gate * sig).astype(BF16)
        gg_ref[places[r], :] = (gh * up * sig * (1.0 + gate * (1.0 - sig))).astype(BF16)

    describe(("far",)).wait_send()
    for i, (_, order, _, _) in enumerate(STREAMS):
        zref = cut(i, c, 0 if order == "zx" else slice(None), pl.ds(0, NZ - 1))
        copy(zref, zref, z_s.at[i], z_r.at[i, 0], sib).wait_send()
        xref = cut(i, c, pl.ds(0, 3), pl.ds(0, NZ) if order == "zx" else 0)
        copy(xref, xref, x_s.at[i], x_r.at[i, 0], sib).wait_send()
    half = data.at[c]
    copy(half, half, sib_s, sib_r.at[0], sib).wait_send()
    three = hs.at[pl.ds(0, NCOL - 1)]
    copy(three, three, h_s, h_r.at[0], sib).wait_send()
    copy(rbuf, rbuf, p_s, p_r, sib).wait_send()


def shards(out_grad, down_weight, block_mask, gate_act, up_act):
    vmem = pl.BlockSpec(memory_space=pltpu.VMEM)
    hbm = pl.BlockSpec(memory_space=pl.ANY)
    dma = pltpu.SemaphoreType.DMA
    units = down_weight.shape[0]
    n = len(STREAMS)
    scratch = [
        pltpu.VMEM(out_grad.shape, BF16),
        pltpu.VMEM(down_weight.shape, BF16),
        pltpu.SMEM(block_mask.shape, jnp.int32),
        pltpu.VMEM(gate_act.shape, BF16),
        pltpu.VMEM(up_act.shape, BF16),
        pltpu.VMEM((NC, NX, NZ, NH, PACK, HALF), BF16),
        pltpu.VMEM((2 * units, HALF), BF16),
        pltpu.VMEM((NX, NZ, ROWS, units), BF16),
        pltpu.VMEM((2 * units, HALF), F32),
        pltpu.VMEM((NX, NZ, ROWS, units), F32),
        pltpu.VMEM((NX, NZ, ROWS, units), BF16),
        pltpu.VMEM((NCOL - 1, NZ, ROWS, units), BF16),
        dma((5,)), dma, dma, dma((n,)), dma((n, 2 * STEPS)), dma((n,)), dma((n, 3 * GROUPS)),
        dma, dma((GROUPS,)), dma, dma((NCOL - 1,)), dma, dma,
    ]
    return pl.pallas_call(
        kernel,
        out_shape=(
            jax.ShapeDtypeStruct(gate_act.shape, BF16),
            jax.ShapeDtypeStruct(up_act.shape, BF16),
            jax.ShapeDtypeStruct(down_weight.shape, BF16),
        ),
        in_specs=[hbm] * 5,
        out_specs=(vmem, vmem, vmem),
        scratch_shapes=scratch,
        compiler_params=pltpu.CompilerParams(
            collective_id=0, has_side_effects=True, vmem_limit_bytes=56 * 1024 * 1024
        ),
    )(out_grad, down_weight, block_mask, gate_act, up_act)


def solution(mesh):
    in_specs = (P("row", "col"), P("row", "col"), P("row", "col"), P("col", "row"), P("col", "row"))
    out_specs = (P("col", "row"), P("col", "row"), P("row", "col"))
    return jax.shard_map(shards, mesh=mesh, in_specs=in_specs, out_specs=out_specs, check_vma=False)
```

```python
import heapq

import jax
import jax.numpy as jnp
from jax import lax
from jax.experimental import pallas as pl
from jax.experimental.pallas import tpu as pltpu
from jax.sharding import PartitionSpec as P

MESH = pl.DeviceIdType.MESH
F32 = jnp.float32
BF16 = jnp.bfloat16

BLK = 128
NX, NZ, NH, NC, NCOL = 4, 12, 2, 2, 4
TOK = 8
PACK = 2 * TOK
HALF = 1024
ROWS = NH * NC * TOK
STEPS = NZ // 2
GROUPS = ((0, 1), (1, 5), (5, 9), (9, 12))
VMEM_LIMIT = 56 * 1024 * 1024
WAYS = (STEPS, STEPS - 1)

STREAMS = (
    (0, "zx", 256, 768),
    (0, "xz", 0, 256),
    (1, "zx", 256, 768),
    (1, "xz", 0, 256),
)


XCOUNT = [3 * len(GROUPS) if order == "zx" else 3 for _, order, _, _ in STREAMS]


def slots(g):
    return GROUPS[g]


def slot_offset(r):
    if r == 0:
        return 0
    if r == NZ - 1:
        return STEPS
    s = (r + 1) // 2
    return -s if r % 2 else s


def group_of(s):
    lo = 2 * s - 1
    g = next(g for g, (a, b) in enumerate(GROUPS) if a <= lo < b)
    return g, GROUPS[g][1] - GROUPS[g][0]


def make_plan(latency=3.2, hidden_at=16.0, slack=1.0, far_at=5.0):
    rate = {"z": 91e3, "x": 91e3, "sib": 300e3}
    free = {"z": 0.0, "x": 0.0, "sib": 0.0}
    issue, product = 0.08, 0.6
    ops, arrivals = [], []
    now = 0.0
    seen = {}
    ready = [0] * len(GROUPS)
    todo = []

    def start(msg, kind, size, hops=1):
        nonlocal now
        ops.append(("start", msg))
        now += issue
        free[kind] = max(free[kind], now) + size * hops / rate[kind]
        late = latency if kind != "sib" else 1.0 + slack
        heapq.heappush(arrivals, (free[kind] + late, msg))

    def size(i, slots_, xs):
        return slots_ * xs * PACK * STREAMS[i][3] * 2

    def nslots(g):
        lo, hi = slots(g)
        return hi - lo

    def send_z(i, s, ways=(0, 1)):
        for t in (s + 2, s + 1):
            for way in ways:
                if t <= WAYS[way]:
                    xs = 1 if STREAMS[i][1] == "zx" else NX
                    start(("z", i, way, t), "z", size(i, 1, xs), t - s)

    def send_x(i, g, k):
        start(("x", i, g, k), "x", size(i, nslots(g), 1))

    def send_sib(i, g, k):
        start(("sib", i, g, k), "sib", size(i, nslots(g), NX if k is None else 1))

    def begin(i):
        if STREAMS[i][1] == "zx":
            send_z(i, 0)
        send_x(i, 0, 0)
        send_x(i, 0, 2)
        if STREAMS[i][1] == "zx":
            send_sib(i, 0, 3)

    def count(key, full):
        seen[key] = seen.get(key, 0) + 1
        return seen[key] == full

    for i, stream in enumerate(STREAMS):
        if stream[0] == 0:
            begin(i)
    ops.append(("prepare",))
    now += 1.5
    heapq.heappush(arrivals, (far_at, ("far",)))
    heapq.heappush(arrivals, (hidden_at, ("hid",)))
    pieces = sum(4 if order == "zx" else 1 for _, order, _, _ in STREAMS)
    late = []
    while arrivals or todo:
        if todo and (not arrivals or arrivals[0][0] > now):
            todo.sort(key=lambda task: task[0] != "term")
            ops.append(todo.pop(0))
            now += product
            continue
        at, msg = heapq.heappop(arrivals)
        now = max(now, at) + issue
        if msg[0] == "sib":
            g = msg[2]
            ready[g] += 1
            if ready[g] == pieces:
                todo.append(("term", g))
                (todo if seen.get("hid") else late).append(("wgrad", g))
            continue
        ops.append(("wait", msg))
        if msg[0] == "far":
            for i, stream in enumerate(STREAMS):
                if stream[0] == 1:
                    begin(i)
        elif msg[0] == "hid":
            seen["hid"] = 1
            todo += late
        elif msg[0] == "z":
            _, i, way, s = msg
            if s % 2 == 0:
                send_z(i, s, (way,))
            g, full = group_of(s)
            if count(("z", i, g), full):
                if STREAMS[i][1] == "zx":
                    send_x(i, g, 0)
                    send_x(i, g, 2)
                    send_sib(i, g, 3)
                else:
                    send_sib(i, g, None)
        else:
            _, i, g, k = msg
            if k == 0:
                send_x(i, g, 1)
            if STREAMS[i][1] == "zx":
                send_sib(i, g, k)
            elif count(("x", i, g), 3):
                send_z(i, 0)
                send_sib(i, g, None)
    return ops, now


def kernel(
    x_hbm, w_hbm, mask_hbm, gate_hbm, up_hbm,
    gg_ref, gu_ref, gd_ref,
    xv, wv, mask, gv, uv, data, wm, hs, acc, tbuf, pbuf, rbuf,
    in_s, far_s, far_r, z_s, z_r, x_s, x_r, sib_s, sib_r, h_s, h_r, p_s, p_r,
):
    row, col = lax.axis_index("row"), lax.axis_index("col")
    c = lax.rem(row, NC)
    h = lax.rem(row // NC, NH)
    z0 = lax.rem(row // (NC * NH), NZ)
    x0 = row // (NC * NH * NZ)
    d = 1 - 2 * c
    xprev, xnext = lax.rem(x0 - d + NX, NX), lax.rem(x0 + d + NX, NX)

    def device(x, z, hh, cc):
        return (((x * NZ + z) * NH + hh) * NC + cc, col)

    xf = device(xnext, z0, h, c)
    xb = device(xprev, z0, h, c)
    zw = [[device(x0, lax.rem(z0 + t * e + NZ, NZ), h, c) for t in (1, 2)] for e in (d, -d)]
    sib = device(x0, z0, h, 1 - c)
    far = device(x0, z0, 1 - h, c)
    cols = [(row, lax.rem(col + k, NCOL)) for k in range(1, NCOL)]

    def copy(src, dst, send, recv, to):
        return pltpu.make_async_remote_copy(
            src_ref=src, dst_ref=dst, send_sem=send, recv_sem=recv,
            device_id=to, device_id_type=MESH,
        )

    barrier = pltpu.get_barrier_semaphore()
    peers = [xf, xb, *zw[0], *zw[1], sib, far] + cols
    loads = [
        pltpu.make_async_copy(src, dst, in_s.at[k])
        for k, (src, dst) in enumerate(
            ((x_hbm, xv), (w_hbm, wv), (mask_hbm, mask), (gate_hbm, gv), (up_hbm, uv))
        )
    ]
    loads[0].start()
    for peer in peers:
        pl.semaphore_signal(barrier, inc=1, device_id=peer, device_id_type=MESH)
    for load in loads[1:]:
        load.start()
    loads[0].wait()
    xs = xv[...].astype(F32)
    data[c, x0, 0, h] = jnp.concatenate([xs[:, :HALF], xs[:, HALF:]], axis=0).astype(BF16)
    pl.semaphore_wait(barrier, len(peers))

    def zslot(way, s):
        if s == 0:
            return 0
        if s == STEPS:
            return NZ - 1
        return 2 * s - 1 + c if way == 0 else 2 * s - c

    def cut(i, core, xsel, rsel):
        whose, _, lane, n = STREAMS[i]
        return data.at[core, xsel, rsel, h if whose == 0 else 1 - h, :, pl.ds(lane, n)]

    def span(g):
        lo, hi = slots(g)
        return pl.ds(lo, hi - lo)

    xsem = [sum(XCOUNT[:i]) for i in range(len(STREAMS))]

    def describe(msg):
        kind = msg[0]
        if kind == "far":
            ref = data.at[c, x0, 0, h]
            return copy(ref, ref, far_s, far_r, far)
        if kind == "hid":
            ref = hs.at[col]
            return copy(ref, ref, h_s, h_r.at[msg[1]], cols[msg[1]])
        if kind == "part":
            _, g, k = msg
            src = pbuf.at[lax.rem(col + k + 1, NCOL), span(g)]
            return copy(src, rbuf.at[k, span(g)], p_s, p_r, cols[k])
        if kind == "z":
            _, i, way, s = msg
            xsel = x0 if STREAMS[i][1] == "zx" else slice(None)
            hops = 2 - s % 2
            src, dst = cut(i, c, xsel, zslot(way, s - hops)), cut(i, c, xsel, zslot(way, s))
            return copy(src, dst, z_s.at[i], z_r.at[i, way * STEPS + s - 1], zw[way][hops - 1])
        if kind == "x":
            _, i, g, k = msg
            ref = cut(i, c, xprev if k == 1 else x0, span(g))
            return copy(ref, ref, x_s.at[i], x_r.at[xsem[i] + 3 * g + k], xb if k == 2 else xf)
        _, i, g, k = msg
        xsel = slice(None) if k is None else (xprev, lax.rem(x0 + 2, NX), xnext, x0)[k]
        ref = cut(i, c, xsel, span(g))
        return copy(ref, ref, sib_s, sib_r.at[g], sib)

    def blocks(g):
        lo, hi = slots(g)
        return [data[cc, :, lo:hi].reshape(NX * (hi - lo) * NH * PACK, HALF) for cc in range(NC)]

    def term(g):
        ref = data.at[1 - c, :, span(g)]
        copy(ref, ref, sib_s, sib_r.at[g], sib).wait_recv()
        lo, hi = slots(g)
        terms = []
        for block in blocks(g):
            t = lax.dot_general(
                block, wm[...], (((1,), (1,)), ((), ())), preferred_element_type=F32
            ).reshape(NX, hi - lo, NH, 2, TOK, 2 * BLK)
            terms.append(t[:, :, :, 0, :, :BLK] + t[:, :, :, 1, :, BLK:])
        value = jnp.concatenate(terms, axis=-2).reshape(NX, hi - lo, ROWS, BLK)
        tbuf[:, lo:hi] = value
        pbuf[:, lo:hi] = value.astype(BF16)
        for k in range(NCOL - 1):
            describe(("part", g, k)).start()

    started = []

    def wgrad(g):
        lo, hi = slots(g)
        hid = hs[:, lo:hi].astype(F32).reshape(NX, hi - lo, NH, NC, TOK, BLK)
        hids = []
        for cc in range(NC):
            v = hid[:, :, :, cc]
            zero = jnp.zeros_like(v)
            both = jnp.concatenate(
                [jnp.concatenate([v, zero], axis=-1), jnp.concatenate([zero, v], axis=-1)], axis=-2
            )
            hids.append(both.reshape(-1, 2 * BLK).astype(BF16))
        t = lax.dot_general(
            jnp.concatenate(hids, axis=0), jnp.concatenate(blocks(g), axis=0),
            (((0,), (0,)), ((), ())), preferred_element_type=F32,
        )
        acc[...] = acc[...] + t if started else t
        started.append(g)

    places = []
    for r in range(NZ):
        z = lax.rem(z0 + slot_offset(r) + NZ, NZ)
        places.append(pl.ds(pl.multiple_of(z * ROWS, ROWS), ROWS))

    def prepare():
        loads[3].wait()
        loads[4].wait()
        for r in range(NZ):
            gate = gv[places[r], :].astype(F32)
            up = uv[places[r], :].astype(F32)
            hs[col, r] = (gate * jax.nn.sigmoid(gate) * up).astype(BF16)
        for k in range(NCOL - 1):
            describe(("hid", k)).start()
        loads[1].wait()
        loads[2].wait()
        for b in range(2 * HALF // BLK):
            part, at = divmod(b * BLK, HALF)
            scale = mask[0, b].astype(F32)
            value = wv[:, b * BLK:(b + 1) * BLK].astype(F32) * scale
            wm[part * BLK:(part + 1) * BLK, at:at + BLK] = value.astype(BF16)

    describe(("far",)).start()
    for op in make_plan()[0]:
        if op[0] == "prepare":
            prepare()
        elif op[0] == "term":
            term(op[1])
        elif op[0] == "wgrad":
            wgrad(op[1])
        elif op[0] == "start":
            describe(op[1]).start()
        elif op[1][0] == "hid":
            for k in range(NCOL - 1):
                describe(("hid", k)).wait_recv()
        else:
            describe(op[1]).wait_recv()

    for b in range(2 * HALF // BLK):
        part, at = divmod(b * BLK, HALF)
        scale = mask[0, b].astype(F32)
        value = acc[part * BLK:(part + 1) * BLK, at:at + BLK] * scale
        gd_ref[:, b * BLK:(b + 1) * BLK] = value.astype(BF16)
    copy(rbuf, rbuf, p_s, p_r, sib).wait_recv()
    for r in range(NZ):
        gate = gv[places[r], :].astype(F32)
        up = uv[places[r], :].astype(F32)
        sig = jax.nn.sigmoid(gate)
        gh = tbuf[col, r]
        for k in range(NCOL - 1):
            gh = gh + rbuf[k, r].astype(F32)
        gu_ref[places[r], :] = (gh * gate * sig).astype(BF16)
        gg_ref[places[r], :] = (gh * up * sig * (1.0 + gate * (1.0 - sig))).astype(BF16)

    describe(("far",)).wait_send()
    for i, (_, order, _, _) in enumerate(STREAMS):
        zref = cut(i, c, 0 if order == "zx" else slice(None), pl.ds(0, NZ - 1))
        copy(zref, zref, z_s.at[i], z_r.at[i, 0], sib).wait_send()
        xref = cut(i, c, pl.ds(0, 3), pl.ds(0, NZ) if order == "zx" else 0)
        copy(xref, xref, x_s.at[i], x_r.at[0], sib).wait_send()
    half = data.at[c]
    copy(half, half, sib_s, sib_r.at[0], sib).wait_send()
    three = hs.at[pl.ds(0, NCOL - 1)]
    copy(three, three, h_s, h_r.at[0], sib).wait_send()
    copy(rbuf, rbuf, p_s, p_r, sib).wait_send()


def shards(out_grad, down_weight, block_mask, gate_act, up_act):
    vmem = pl.BlockSpec(memory_space=pltpu.VMEM)
    hbm = pl.BlockSpec(memory_space=pl.ANY)
    dma = pltpu.SemaphoreType.DMA
    units = down_weight.shape[0]
    n = len(STREAMS)
    xcount = sum(XCOUNT)
    scratch = [
        pltpu.VMEM(out_grad.shape, BF16),
        pltpu.VMEM(down_weight.shape, BF16),
        pltpu.SMEM(block_mask.shape, jnp.int32),
        pltpu.VMEM(gate_act.shape, BF16),
        pltpu.VMEM(up_act.shape, BF16),
        pltpu.VMEM((NC, NX, NZ, NH, PACK, HALF), BF16),
        pltpu.VMEM((2 * units, HALF), BF16),
        pltpu.VMEM((NX, NZ, ROWS, units), BF16),
        pltpu.VMEM((2 * units, HALF), F32),
        pltpu.VMEM((NX, NZ, ROWS, units), F32),
        pltpu.VMEM((NX, NZ, ROWS, units), BF16),
        pltpu.VMEM((NCOL - 1, NZ, ROWS, units), BF16),
        dma((5,)), dma, dma, dma((n,)), dma((n, 2 * STEPS - 1)), dma((n,)), dma((xcount,)),
        dma, dma((len(GROUPS),)), dma, dma((NCOL - 1,)), dma, dma,
    ]
    out_shape = (
        jax.ShapeDtypeStruct(gate_act.shape, BF16),
        jax.ShapeDtypeStruct(up_act.shape, BF16),
        jax.ShapeDtypeStruct(down_weight.shape, BF16),
    )
    return pl.pallas_call(
        kernel,
        out_shape=out_shape,
        in_specs=[hbm] * 5,
        out_specs=(vmem, vmem, vmem),
        scratch_shapes=scratch,
        compiler_params=pltpu.CompilerParams(
            collective_id=0, has_side_effects=True, vmem_limit_bytes=VMEM_LIMIT
        ),
    )(out_grad, down_weight, block_mask, gate_act, up_act)


def solution(mesh):
    in_specs = (P("row", "col"), P("row", "col"), P("row", "col"), P("col", "row"), P("col", "row"))
    out_specs = (P("col", "row"), P("col", "row"), P("row", "col"))
    return jax.shard_map(shards, mesh=mesh, in_specs=in_specs, out_specs=out_specs, check_vma=False)
```

```python
import heapq

import jax
import jax.numpy as jnp
from jax import lax
from jax.experimental import pallas as pl
from jax.experimental.pallas import tpu as pltpu
from jax.sharding import PartitionSpec as P

MESH = pl.DeviceIdType.MESH
F32 = jnp.float32
BF16 = jnp.bfloat16

BLK = 128
NX, NZ, NH, NC, NCOL = 4, 12, 2, 2, 4
TOK = 8
PACK = 2 * TOK
HALF = 1024
ROWS = NH * NC * TOK
STEPS = NZ // 2
GROUPS = ((0, 1), (1, 3), (3, 5), (5, 7), (7, 9), (9, 11), (11, 12))
VMEM_LIMIT = 56 * 1024 * 1024
WAYS = (STEPS, STEPS - 1)

RING = (0, 1, 2, 3, 4, 5)
SKIP = (0, 0, 2, 2, 4, 4)
MIXED = (0, 0, 2, 2, 4, 5)

STREAMS = (
    (0, "zx", 256, 768, MIXED),
    (0, "xz", 0, 256, RING),
    (1, "zx", 256, 768, SKIP),
    (1, "xz", 0, 256, SKIP),
)
XCOUNT = [3 * len(GROUPS) if order == "zx" else 3 for _, order, _, _, _ in STREAMS]


def slots(g):
    return GROUPS[g]


def slot_offset(r):
    if r == 0:
        return 0
    if r == NZ - 1:
        return STEPS
    s = (r + 1) // 2
    return -s if r % 2 else s


def group_of(s):
    lo = 2 * s - 1
    g = next(g for g, (a, b) in enumerate(GROUPS) if a <= lo < b)
    return g, GROUPS[g][1] - GROUPS[g][0]


def make_plan(latency=3.2, hidden_at=16.0, slack=0.5, far_at=5.0):
    rate = {"z": 91e3, "x": 91e3, "sib": 300e3}
    free = {"z": 0.0, "x": 0.0, "sib": 0.0}
    issue = 0.02
    ops, arrivals = [], []
    now = 0.0
    seen = {}
    ready = [0] * len(GROUPS)
    todo = []

    def start(msg, kind, size, hops=1):
        nonlocal now
        ops.append(("start", msg))
        now += issue
        free[kind] = max(free[kind], now) + size * hops / rate[kind]
        late = latency if kind != "sib" else 1.0 + slack
        heapq.heappush(arrivals, (free[kind] + late, msg))

    def size(i, slots_, xs):
        return slots_ * xs * PACK * STREAMS[i][3] * 2

    def nslots(g):
        lo, hi = slots(g)
        return hi - lo

    def send_z(i, s, ways=(0, 1)):
        for t in range(STEPS, 0, -1):
            for way in ways:
                if STREAMS[i][4][t - 1] == s and t <= WAYS[way]:
                    xs = 1 if STREAMS[i][1] == "zx" else NX
                    start(("z", i, way, t), "z", size(i, 1, xs), t - s)

    def send_x(i, g, k):
        start(("x", i, g, k), "x", size(i, nslots(g), 1))

    def send_sib(i, g, k):
        start(("sib", i, g, k), "sib", size(i, nslots(g), NX if k is None else 1))

    def begin(i):
        if STREAMS[i][1] == "zx":
            send_z(i, 0)
        send_x(i, 0, 0)
        send_x(i, 0, 2)
        if STREAMS[i][1] == "zx":
            send_sib(i, 0, 3)

    def count(key, full):
        seen[key] = seen.get(key, 0) + 1
        return seen[key] == full

    for i, stream in enumerate(STREAMS):
        if stream[0] == 0:
            begin(i)
    ops.append(("prepare",))
    now += 1.0
    heapq.heappush(arrivals, (far_at, ("far",)))
    heapq.heappush(arrivals, (hidden_at, ("hid",)))
    pieces = sum(4 if order == "zx" else 1 for _, order, _, _, _ in STREAMS)
    late = []
    while arrivals or todo:
        if todo and (not arrivals or arrivals[0][0] > now):
            todo.sort(key=lambda task: task[0] != "term")
            ops.append(todo.pop(0))
            now += 0.1 + 0.08 * nslots(ops[-1][1])
            continue
        at, msg = heapq.heappop(arrivals)
        now = max(now, at) + issue
        if msg[0] == "sib":
            g = msg[2]
            ready[g] += 1
            if ready[g] == pieces:
                todo.append(("term", g))
                (todo if seen.get("hid") else late).append(("wgrad", g))
            continue
        ops.append(("wait", msg))
        if msg[0] == "far":
            ops.extend(("start", ("hid", k)) for k in range(NCOL - 1))
            for i, stream in enumerate(STREAMS):
                if stream[0] == 1:
                    begin(i)
        elif msg[0] == "hid":
            seen["hid"] = 1
            todo += late
        elif msg[0] == "z":
            _, i, way, s = msg
            send_z(i, s, (way,))
            g, full = group_of(s)
            if count(("z", i, g), full):
                if STREAMS[i][1] == "zx":
                    send_x(i, g, 0)
                    send_x(i, g, 2)
                    send_sib(i, g, 3)
                else:
                    send_sib(i, g, None)
        else:
            _, i, g, k = msg
            if k == 0:
                send_x(i, g, 1)
            if STREAMS[i][1] == "zx":
                send_sib(i, g, k)
            elif count(("x", i, g), 3):
                send_z(i, 0)
                send_sib(i, g, None)
    return ops, now


def kernel(
    x_hbm, w_hbm, mask_hbm, gate_hbm, up_hbm,
    gg_ref, gu_ref, gd_ref,
    xv, wv, mask, gv, uv, data, wm, hs, acc, tbuf, pbuf, rbuf,
    in_s, far_s, far_r, z_s, z_r, x_s, x_r, sib_s, sib_r, h_s, h_r, p_s, p_r,
):
    row, col = lax.axis_index("row"), lax.axis_index("col")
    c = lax.rem(row, NC)
    h = lax.rem(row // NC, NH)
    z0 = lax.rem(row // (NC * NH), NZ)
    x0 = row // (NC * NH * NZ)
    d = 1 - 2 * c
    xprev, xnext = lax.rem(x0 - d + NX, NX), lax.rem(x0 + d + NX, NX)

    def device(x, z, hh, cc):
        return (((x * NZ + z) * NH + hh) * NC + cc, col)

    xf = device(xnext, z0, h, c)
    xb = device(xprev, z0, h, c)
    zw = [[device(x0, lax.rem(z0 + t * e + NZ, NZ), h, c) for t in (1, 2)] for e in (d, -d)]
    sib = device(x0, z0, h, 1 - c)
    far = device(x0, z0, 1 - h, c)
    cols = [(row, lax.rem(col + k, NCOL)) for k in range(1, NCOL)]

    def copy(src, dst, send, recv, to):
        return pltpu.make_async_remote_copy(
            src_ref=src, dst_ref=dst, send_sem=send, recv_sem=recv,
            device_id=to, device_id_type=MESH,
        )

    barrier = pltpu.get_barrier_semaphore()
    peers = [xf, xb, *zw[0], *zw[1], sib, far] + cols
    loads = [
        pltpu.make_async_copy(src, dst, in_s.at[k])
        for k, (src, dst) in enumerate(
            ((x_hbm, xv), (w_hbm, wv), (mask_hbm, mask), (gate_hbm, gv), (up_hbm, uv))
        )
    ]
    loads[0].start()
    for peer in peers:
        pl.semaphore_signal(barrier, inc=1, device_id=peer, device_id_type=MESH)
    for load in loads[1:]:
        load.start()
    loads[0].wait()
    xs = xv[...].astype(F32)
    data[c, x0, 0, h] = jnp.concatenate([xs[:, :HALF], xs[:, HALF:]], axis=0).astype(BF16)
    pl.semaphore_wait(barrier, len(peers))

    def zslot(way, s):
        if s == 0:
            return 0
        if s == STEPS:
            return NZ - 1
        return 2 * s - 1 + c if way == 0 else 2 * s - c

    def cut(i, core, xsel, rsel):
        whose, _, lane, n, _ = STREAMS[i]
        return data.at[core, xsel, rsel, h if whose == 0 else 1 - h, :, pl.ds(lane, n)]

    def span(g):
        lo, hi = slots(g)
        return pl.ds(lo, hi - lo)

    xsem = [sum(XCOUNT[:i]) for i in range(len(STREAMS))]

    def describe(msg):
        kind = msg[0]
        if kind == "far":
            ref = data.at[c, x0, 0, h]
            return copy(ref, ref, far_s, far_r, far)
        if kind == "hid":
            ref = hs.at[col]
            return copy(ref, ref, h_s, h_r.at[msg[1]], cols[msg[1]])
        if kind == "part":
            _, g, k = msg
            src = pbuf.at[lax.rem(col + k + 1, NCOL), span(g)]
            return copy(src, rbuf.at[k, span(g)], p_s, p_r, cols[k])
        if kind == "z":
            _, i, way, s = msg
            xsel = x0 if STREAMS[i][1] == "zx" else slice(None)
            hops = s - STREAMS[i][4][s - 1]
            src, dst = cut(i, c, xsel, zslot(way, s - hops)), cut(i, c, xsel, zslot(way, s))
            return copy(src, dst, z_s.at[i], z_r.at[i, way * STEPS + s - 1], zw[way][hops - 1])
        if kind == "x":
            _, i, g, k = msg
            ref = cut(i, c, xprev if k == 1 else x0, span(g))
            return copy(ref, ref, x_s.at[i], x_r.at[xsem[i] + 3 * g + k], xb if k == 2 else xf)
        _, i, g, k = msg
        xsel = slice(None) if k is None else (xprev, lax.rem(x0 + 2, NX), xnext, x0)[k]
        ref = cut(i, c, xsel, span(g))
        return copy(ref, ref, sib_s, sib_r.at[g], sib)

    def blocks(g):
        lo, hi = slots(g)
        return [data[cc, :, lo:hi].reshape(NX * (hi - lo) * NH * PACK, HALF) for cc in range(NC)]

    def term(g):
        ref = data.at[1 - c, :, span(g)]
        copy(ref, ref, sib_s, sib_r.at[g], sib).wait_recv()
        lo, hi = slots(g)
        terms = []
        for block in blocks(g):
            t = lax.dot_general(
                block, wm[...], (((1,), (1,)), ((), ())), preferred_element_type=F32
            ).reshape(NX, hi - lo, NH, 2, TOK, 2 * BLK)
            terms.append(t[:, :, :, 0, :, :BLK] + t[:, :, :, 1, :, BLK:])
        value = jnp.concatenate(terms, axis=-2).reshape(NX, hi - lo, ROWS, BLK)
        tbuf[:, lo:hi] = value
        pbuf[:, lo:hi] = value.astype(BF16)
        for k in range(NCOL - 1):
            describe(("part", g, k)).start()

    started = []

    def wgrad(g):
        lo, hi = slots(g)
        hid = hs[:, lo:hi].astype(F32).reshape(NX, hi - lo, NH, NC, TOK, BLK)
        hids = []
        for cc in range(NC):
            v = hid[:, :, :, cc]
            zero = jnp.zeros_like(v)
            both = jnp.concatenate(
                [jnp.concatenate([v, zero], axis=-1), jnp.concatenate([zero, v], axis=-1)], axis=-2
            )
            hids.append(both.reshape(-1, 2 * BLK).astype(BF16))
        t = lax.dot_general(
            jnp.concatenate(hids, axis=0), jnp.concatenate(blocks(g), axis=0),
            (((0,), (0,)), ((), ())), preferred_element_type=F32,
        )
        acc[...] = acc[...] + t if started else t
        started.append(g)

    places = []
    for r in range(NZ):
        z = lax.rem(z0 + slot_offset(r) + NZ, NZ)
        places.append(pl.ds(pl.multiple_of(z * ROWS, ROWS), ROWS))

    def prepare():
        loads[3].wait()
        loads[4].wait()
        for r in range(NZ):
            gate = gv[places[r], :].astype(F32)
            up = uv[places[r], :].astype(F32)
            hs[col, r] = (gate * jax.nn.sigmoid(gate) * up).astype(BF16)
        loads[1].wait()
        loads[2].wait()
        for b in range(2 * HALF // BLK):
            part, at = divmod(b * BLK, HALF)
            scale = mask[0, b].astype(F32)
            value = wv[:, b * BLK:(b + 1) * BLK].astype(F32) * scale
            wm[part * BLK:(part + 1) * BLK, at:at + BLK] = value.astype(BF16)

    describe(("far",)).start()
    for op in make_plan()[0]:
        if op[0] == "prepare":
            prepare()
        elif op[0] == "term":
            term(op[1])
        elif op[0] == "wgrad":
            wgrad(op[1])
        elif op[0] == "start":
            describe(op[1]).start()
        elif op[1][0] == "hid":
            for k in range(NCOL - 1):
                describe(("hid", k)).wait_recv()
        else:
            describe(op[1]).wait_recv()

    for b in range(2 * HALF // BLK):
        part, at = divmod(b * BLK, HALF)
        scale = mask[0, b].astype(F32)
        value = acc[part * BLK:(part + 1) * BLK, at:at + BLK] * scale
        gd_ref[:, b * BLK:(b + 1) * BLK] = value.astype(BF16)
    copy(rbuf, rbuf, p_s, p_r, sib).wait_recv()
    for r in range(NZ):
        gate = gv[places[r], :].astype(F32)
        up = uv[places[r], :].astype(F32)
        sig = jax.nn.sigmoid(gate)
        gh = tbuf[col, r]
        for k in range(NCOL - 1):
            gh = gh + rbuf[k, r].astype(F32)
        gu_ref[places[r], :] = (gh * gate * sig).astype(BF16)
        gg_ref[places[r], :] = (gh * up * sig * (1.0 + gate * (1.0 - sig))).astype(BF16)

    describe(("far",)).wait_send()
    for i, (_, order, _, _, _) in enumerate(STREAMS):
        zref = cut(i, c, 0 if order == "zx" else slice(None), pl.ds(0, NZ - 1))
        copy(zref, zref, z_s.at[i], z_r.at[i, 0], sib).wait_send()
        xref = cut(i, c, pl.ds(0, 3), pl.ds(0, NZ) if order == "zx" else 0)
        copy(xref, xref, x_s.at[i], x_r.at[0], sib).wait_send()
    half = data.at[c]
    copy(half, half, sib_s, sib_r.at[0], sib).wait_send()
    three = hs.at[pl.ds(0, NCOL - 1)]
    copy(three, three, h_s, h_r.at[0], sib).wait_send()
    copy(rbuf, rbuf, p_s, p_r, sib).wait_send()


def hand_over(*refs):
    for src, dst in zip(refs[:3], refs[3:]):
        dst[...] = src[...]


def shards(out_grad, down_weight, block_mask, gate_act, up_act):
    vmem = pl.BlockSpec(memory_space=pltpu.VMEM)
    hbm = pl.BlockSpec(memory_space=pl.ANY)
    dma = pltpu.SemaphoreType.DMA
    units = down_weight.shape[0]
    n = len(STREAMS)
    xcount = sum(XCOUNT)
    scratch = [
        pltpu.VMEM(out_grad.shape, BF16),
        pltpu.VMEM(down_weight.shape, BF16),
        pltpu.SMEM(block_mask.shape, jnp.int32),
        pltpu.VMEM(gate_act.shape, BF16),
        pltpu.VMEM(up_act.shape, BF16),
        pltpu.VMEM((NC, NX, NZ, NH, PACK, HALF), BF16),
        pltpu.VMEM((2 * units, HALF), BF16),
        pltpu.VMEM((NX, NZ, ROWS, units), BF16),
        pltpu.VMEM((2 * units, HALF), F32),
        pltpu.VMEM((NX, NZ, ROWS, units), F32),
        pltpu.VMEM((NX, NZ, ROWS, units), BF16),
        pltpu.VMEM((NCOL - 1, NZ, ROWS, units), BF16),
        dma((5,)), dma, dma, dma((n,)), dma((n, 2 * STEPS - 1)), dma((n,)), dma((xcount,)),
        dma, dma((len(GROUPS),)), dma, dma((NCOL - 1,)), dma, dma,
    ]
    out_shape = (
        jax.ShapeDtypeStruct(gate_act.shape, BF16),
        jax.ShapeDtypeStruct(up_act.shape, BF16),
        jax.ShapeDtypeStruct(down_weight.shape, BF16),
    )
    results = pl.pallas_call(
        kernel,
        out_shape=out_shape,
        in_specs=[hbm] * 5,
        out_specs=(vmem, vmem, vmem),
        scratch_shapes=scratch,
        compiler_params=pltpu.CompilerParams(
            collective_id=0, has_side_effects=True, vmem_limit_bytes=VMEM_LIMIT
        ),
    )(out_grad, down_weight, block_mask, gate_act, up_act)
    return pl.pallas_call(
        hand_over,
        out_shape=out_shape,
        in_specs=[vmem] * 3,
        out_specs=(vmem,) * 3,
        compiler_params=pltpu.CompilerParams(vmem_limit_bytes=VMEM_LIMIT),
    )(*results)


def solution(mesh):
    in_specs = (P("row", "col"), P("row", "col"), P("row", "col"), P("col", "row"), P("col", "row"))
    out_specs = (P("col", "row"), P("col", "row"), P("row", "col"))
    return jax.shard_map(shards, mesh=mesh, in_specs=in_specs, out_specs=out_specs, check_vma=False)
```

```python
import heapq

import jax
import jax.numpy as jnp
from jax import lax
from jax.experimental import pallas as pl
from jax.experimental.pallas import tpu as pltpu
from jax.sharding import PartitionSpec as P

MESH = pl.DeviceIdType.MESH
F32 = jnp.float32
BF16 = jnp.bfloat16

BLK = 128
NX, NZ, NH, NC, NCOL = 4, 12, 2, 2, 4
TOK = 8
PACK = 2 * TOK
HALF = 1024
ROWS = NH * NC * TOK
STEPS = NZ // 2
GROUPS = ((0, 1), (1, 3), (3, 5), (5, 7), (7, 9), (9, 11), (11, 12))
VMEM_LIMIT = 56 * 1024 * 1024
WAYS = (STEPS, STEPS - 1)

RING = (0, 1, 2, 3, 4, 5)
SKIP = (0, 0, 2, 2, 4, 4)
MIXED = (0, 1, 2, 2, 4, 4)

STREAMS = (
    (0, "zx", 256, 768, MIXED),
    (0, "xz", 0, 256, MIXED),
    (1, "zx", 256, 768, SKIP),
    (1, "xz", 0, 256, SKIP),
)
XCOUNT = [3 * len(GROUPS) if order == "zx" else 3 for _, order, _, _, _ in STREAMS]


def slots(g):
    return GROUPS[g]


def slot_offset(r):
    if r == 0:
        return 0
    if r == NZ - 1:
        return STEPS
    s = (r + 1) // 2
    return -s if r % 2 else s


def group_of(s):
    lo = 2 * s - 1
    g = next(g for g, (a, b) in enumerate(GROUPS) if a <= lo < b)
    return g, GROUPS[g][1] - GROUPS[g][0]


def make_plan(zlate=3.2, xlate=3.6, zrate=97e3, xrate=102e3, far_at=6.2, hidden_at=17.0, slack=1.4):
    rate = {"z": zrate, "x": xrate, "sib": 300e3}
    free = {"z": 0.0, "x": 0.0, "sib": 0.0}
    late = {"z": zlate, "x": xlate, "sib": 1.0 + slack}
    issue = 0.02
    ops, arrivals = [], []
    now = 0.0
    seen = {}
    ready = [0] * len(GROUPS)
    todo = []

    def start(msg, kind, size, hops=1):
        nonlocal now
        ops.append(("start", msg))
        now += issue
        free[kind] = max(free[kind], now) + size * hops / rate[kind]
        heapq.heappush(arrivals, (free[kind] + late[kind], msg))

    def size(i, slots_, xs):
        return slots_ * xs * PACK * STREAMS[i][3] * 2

    def nslots(g):
        lo, hi = slots(g)
        return hi - lo

    def send_z(i, s, ways=(0, 1)):
        for t in range(STEPS, 0, -1):
            for way in ways:
                if STREAMS[i][4][t - 1] == s and t <= WAYS[way]:
                    xs = 1 if STREAMS[i][1] == "zx" else NX
                    start(("z", i, way, t), "z", size(i, 1, xs), t - s)

    def send_x(i, g, k):
        start(("x", i, g, k), "x", size(i, nslots(g), 1))

    def send_sib(i, g, k):
        start(("sib", i, g, k), "sib", size(i, nslots(g), NX if k is None else 1))

    def begin(i):
        if STREAMS[i][1] == "zx":
            send_z(i, 0)
        send_x(i, 0, 0)
        send_x(i, 0, 2)
        if STREAMS[i][1] == "zx":
            send_sib(i, 0, 3)

    def count(key, full):
        seen[key] = seen.get(key, 0) + 1
        return seen[key] == full

    for i, stream in enumerate(STREAMS):
        if stream[0] == 0:
            begin(i)
    ops.append(("prepare",))
    now += 1.0
    heapq.heappush(arrivals, (far_at, ("far",)))
    heapq.heappush(arrivals, (hidden_at, ("hid",)))
    pieces = sum(4 if order == "zx" else 1 for _, order, _, _, _ in STREAMS)
    waiting = []
    while arrivals or todo:
        if todo and (not arrivals or arrivals[0][0] > now):
            todo.sort(key=lambda task: task[0] != "term")
            ops.append(todo.pop(0))
            now += 0.1 + 0.08 * nslots(ops[-1][1])
            continue
        at, msg = heapq.heappop(arrivals)
        now = max(now, at) + issue
        if msg[0] == "sib":
            g = msg[2]
            ready[g] += 1
            if ready[g] == pieces:
                todo.append(("term", g))
                (todo if seen.get("hid") else waiting).append(("wgrad", g))
            continue
        ops.append(("wait", msg))
        if msg[0] == "far":
            ops.extend(("start", ("hid", k)) for k in range(NCOL - 1))
            for i, stream in enumerate(STREAMS):
                if stream[0] == 1:
                    begin(i)
        elif msg[0] == "hid":
            seen["hid"] = 1
            todo += waiting
        elif msg[0] == "z":
            _, i, way, s = msg
            send_z(i, s, (way,))
            g, full = group_of(s)
            if count(("z", i, g), full):
                if STREAMS[i][1] == "zx":
                    send_x(i, g, 0)
                    send_x(i, g, 2)
                    send_sib(i, g, 3)
                else:
                    send_sib(i, g, None)
        else:
            _, i, g, k = msg
            if k == 0:
                send_x(i, g, 1)
            if STREAMS[i][1] == "zx":
                send_sib(i, g, k)
            elif count(("x", i, g), 3):
                send_z(i, 0)
                send_sib(i, g, None)
    return ops, now


def kernel(
    x_hbm, w_hbm, mask_hbm, gate_hbm, up_hbm,
    gg_ref, gu_ref, gd_ref,
    xv, wv, mask, gv, uv, data, wm, hs, acc, tbuf, pbuf, rbuf,
    in_s, far_s, far_r, z_s, z_r, x_s, x_r, sib_s, sib_r, h_s, h_r, p_s, p_r,
):
    row, col = lax.axis_index("row"), lax.axis_index("col")
    c = lax.rem(row, NC)
    h = lax.rem(row // NC, NH)
    z0 = lax.rem(row // (NC * NH), NZ)
    x0 = row // (NC * NH * NZ)
    d = 1 - 2 * c
    xprev, xnext = lax.rem(x0 - d + NX, NX), lax.rem(x0 + d + NX, NX)

    def device(x, z, hh, cc):
        return (((x * NZ + z) * NH + hh) * NC + cc, col)

    xf = device(xnext, z0, h, c)
    xb = device(xprev, z0, h, c)
    zw = [[device(x0, lax.rem(z0 + t * e + NZ, NZ), h, c) for t in (1, 2)] for e in (d, -d)]
    sib = device(x0, z0, h, 1 - c)
    far = device(x0, z0, 1 - h, c)
    cols = [(row, lax.rem(col + k, NCOL)) for k in range(1, NCOL)]

    def copy(src, dst, send, recv, to):
        return pltpu.make_async_remote_copy(
            src_ref=src, dst_ref=dst, send_sem=send, recv_sem=recv,
            device_id=to, device_id_type=MESH,
        )

    barrier = pltpu.get_barrier_semaphore()
    peers = [xf, xb, *zw[0], *zw[1], sib, far] + cols
    loads = [
        pltpu.make_async_copy(src, dst, in_s.at[k])
        for k, (src, dst) in enumerate(
            ((x_hbm, xv), (w_hbm, wv), (mask_hbm, mask), (gate_hbm, gv), (up_hbm, uv))
        )
    ]
    loads[0].start()
    for peer in peers:
        pl.semaphore_signal(barrier, inc=1, device_id=peer, device_id_type=MESH)
    for load in loads[1:]:
        load.start()
    loads[0].wait()
    xs = xv[...].astype(F32)
    data[c, x0, 0, h] = jnp.concatenate([xs[:, :HALF], xs[:, HALF:]], axis=0).astype(BF16)
    pl.semaphore_wait(barrier, len(peers))

    def zslot(way, s):
        if s == 0:
            return 0
        if s == STEPS:
            return NZ - 1
        return 2 * s - 1 + c if way == 0 else 2 * s - c

    def cut(i, core, xsel, rsel):
        whose, _, lane, n, _ = STREAMS[i]
        return data.at[core, xsel, rsel, h if whose == 0 else 1 - h, :, pl.ds(lane, n)]

    def span(g):
        lo, hi = slots(g)
        return pl.ds(lo, hi - lo)

    xsem = [sum(XCOUNT[:i]) for i in range(len(STREAMS))]

    def describe(msg):
        kind = msg[0]
        if kind == "far":
            ref = data.at[c, x0, 0, h]
            return copy(ref, ref, far_s, far_r, far)
        if kind == "hid":
            ref = hs.at[col]
            return copy(ref, ref, h_s, h_r.at[msg[1]], cols[msg[1]])
        if kind == "part":
            _, g, k = msg
            src = pbuf.at[lax.rem(col + k + 1, NCOL), span(g)]
            return copy(src, rbuf.at[k, span(g)], p_s, p_r, cols[k])
        if kind == "z":
            _, i, way, s = msg
            xsel = x0 if STREAMS[i][1] == "zx" else slice(None)
            hops = s - STREAMS[i][4][s - 1]
            src, dst = cut(i, c, xsel, zslot(way, s - hops)), cut(i, c, xsel, zslot(way, s))
            return copy(src, dst, z_s.at[i], z_r.at[i, way * STEPS + s - 1], zw[way][hops - 1])
        if kind == "x":
            _, i, g, k = msg
            ref = cut(i, c, xprev if k == 1 else x0, span(g))
            return copy(ref, ref, x_s.at[i], x_r.at[xsem[i] + 3 * g + k], xb if k == 2 else xf)
        _, i, g, k = msg
        xsel = slice(None) if k is None else (xprev, lax.rem(x0 + 2, NX), xnext, x0)[k]
        ref = cut(i, c, xsel, span(g))
        return copy(ref, ref, sib_s, sib_r.at[g], sib)

    def blocks(g):
        lo, hi = slots(g)
        return [data[cc, :, lo:hi].reshape(NX * (hi - lo) * NH * PACK, HALF) for cc in range(NC)]

    def term(g):
        ref = data.at[1 - c, :, span(g)]
        copy(ref, ref, sib_s, sib_r.at[g], sib).wait_recv()
        lo, hi = slots(g)
        terms = []
        for block in blocks(g):
            t = lax.dot_general(
                block, wm[...], (((1,), (1,)), ((), ())), preferred_element_type=F32
            ).reshape(NX, hi - lo, NH, 2, TOK, 2 * BLK)
            terms.append(t[:, :, :, 0, :, :BLK] + t[:, :, :, 1, :, BLK:])
        value = jnp.concatenate(terms, axis=-2).reshape(NX, hi - lo, ROWS, BLK)
        tbuf[:, lo:hi] = value
        pbuf[:, lo:hi] = value.astype(BF16)
        for k in range(NCOL - 1):
            describe(("part", g, k)).start()

    started = []

    def wgrad(g):
        lo, hi = slots(g)
        hid = hs[:, lo:hi].astype(F32).reshape(NX, hi - lo, NH, NC, TOK, BLK)
        hids = []
        for cc in range(NC):
            v = hid[:, :, :, cc]
            zero = jnp.zeros_like(v)
            both = jnp.concatenate(
                [jnp.concatenate([v, zero], axis=-1), jnp.concatenate([zero, v], axis=-1)], axis=-2
            )
            hids.append(both.reshape(-1, 2 * BLK).astype(BF16))
        t = lax.dot_general(
            jnp.concatenate(hids, axis=0), jnp.concatenate(blocks(g), axis=0),
            (((0,), (0,)), ((), ())), preferred_element_type=F32,
        )
        acc[...] = acc[...] + t if started else t
        started.append(g)

    places = []
    for r in range(NZ):
        z = lax.rem(z0 + slot_offset(r) + NZ, NZ)
        places.append(pl.ds(pl.multiple_of(z * ROWS, ROWS), ROWS))

    def prepare():
        loads[3].wait()
        loads[4].wait()
        for r in range(NZ):
            gate = gv[places[r], :].astype(F32)
            up = uv[places[r], :].astype(F32)
            hs[col, r] = (gate * jax.nn.sigmoid(gate) * up).astype(BF16)
        loads[1].wait()
        loads[2].wait()
        for b in range(2 * HALF // BLK):
            part, at = divmod(b * BLK, HALF)
            scale = mask[0, b].astype(F32)
            value = wv[:, b * BLK:(b + 1) * BLK].astype(F32) * scale
            wm[part * BLK:(part + 1) * BLK, at:at + BLK] = value.astype(BF16)

    describe(("far",)).start()
    for op in make_plan()[0]:
        if op[0] == "prepare":
            prepare()
        elif op[0] == "term":
            term(op[1])
        elif op[0] == "wgrad":
            wgrad(op[1])
        elif op[0] == "start":
            describe(op[1]).start()
        elif op[1][0] == "hid":
            for k in range(NCOL - 1):
                describe(("hid", k)).wait_recv()
        else:
            describe(op[1]).wait_recv()

    for b in range(2 * HALF // BLK):
        part, at = divmod(b * BLK, HALF)
        scale = mask[0, b].astype(F32)
        value = acc[part * BLK:(part + 1) * BLK, at:at + BLK] * scale
        gd_ref[:, b * BLK:(b + 1) * BLK] = value.astype(BF16)
    copy(rbuf, rbuf, p_s, p_r, sib).wait_recv()
    for r in range(NZ):
        gate = gv[places[r], :].astype(F32)
        up = uv[places[r], :].astype(F32)
        sig = jax.nn.sigmoid(gate)
        gh = tbuf[col, r]
        for k in range(NCOL - 1):
            gh = gh + rbuf[k, r].astype(F32)
        gu_ref[places[r], :] = (gh * gate * sig).astype(BF16)
        gg_ref[places[r], :] = (gh * up * sig * (1.0 + gate * (1.0 - sig))).astype(BF16)

    describe(("far",)).wait_send()
    for i, (_, order, _, _, _) in enumerate(STREAMS):
        zref = cut(i, c, 0 if order == "zx" else slice(None), pl.ds(0, NZ - 1))
        copy(zref, zref, z_s.at[i], z_r.at[i, 0], sib).wait_send()
        xref = cut(i, c, pl.ds(0, 3), pl.ds(0, NZ) if order == "zx" else 0)
        copy(xref, xref, x_s.at[i], x_r.at[0], sib).wait_send()
    half = data.at[c]
    copy(half, half, sib_s, sib_r.at[0], sib).wait_send()
    three = hs.at[pl.ds(0, NCOL - 1)]
    copy(three, three, h_s, h_r.at[0], sib).wait_send()
    copy(rbuf, rbuf, p_s, p_r, sib).wait_send()


def hand_over(*refs):
    for src, dst in zip(refs[:3], refs[3:]):
        dst[...] = src[...]


def shards(out_grad, down_weight, block_mask, gate_act, up_act):
    vmem = pl.BlockSpec(memory_space=pltpu.VMEM)
    hbm = pl.BlockSpec(memory_space=pl.ANY)
    dma = pltpu.SemaphoreType.DMA
    units = down_weight.shape[0]
    n = len(STREAMS)
    xcount = sum(XCOUNT)
    scratch = [
        pltpu.VMEM(out_grad.shape, BF16),
        pltpu.VMEM(down_weight.shape, BF16),
        pltpu.SMEM(block_mask.shape, jnp.int32),
        pltpu.VMEM(gate_act.shape, BF16),
        pltpu.VMEM(up_act.shape, BF16),
        pltpu.VMEM((NC, NX, NZ, NH, PACK, HALF), BF16),
        pltpu.VMEM((2 * units, HALF), BF16),
        pltpu.VMEM((NX, NZ, ROWS, units), BF16),
        pltpu.VMEM((2 * units, HALF), F32),
        pltpu.VMEM((NX, NZ, ROWS, units), F32),
        pltpu.VMEM((NX, NZ, ROWS, units), BF16),
        pltpu.VMEM((NCOL - 1, NZ, ROWS, units), BF16),
        dma((5,)), dma, dma, dma((n,)), dma((n, 2 * STEPS - 1)), dma((n,)), dma((xcount,)),
        dma, dma((len(GROUPS),)), dma, dma((NCOL - 1,)), dma, dma,
    ]
    out_shape = (
        jax.ShapeDtypeStruct(gate_act.shape, BF16),
        jax.ShapeDtypeStruct(up_act.shape, BF16),
        jax.ShapeDtypeStruct(down_weight.shape, BF16),
    )
    results = pl.pallas_call(
        kernel,
        out_shape=out_shape,
        in_specs=[hbm] * 5,
        out_specs=(vmem, vmem, vmem),
        scratch_shapes=scratch,
        compiler_params=pltpu.CompilerParams(
            collective_id=0, has_side_effects=True, vmem_limit_bytes=VMEM_LIMIT
        ),
    )(out_grad, down_weight, block_mask, gate_act, up_act)
    return pl.pallas_call(
        hand_over,
        out_shape=out_shape,
        in_specs=[vmem] * 3,
        out_specs=(vmem,) * 3,
        compiler_params=pltpu.CompilerParams(vmem_limit_bytes=VMEM_LIMIT),
    )(*results)


def solution(mesh):
    in_specs = (P("row", "col"), P("row", "col"), P("row", "col"), P("col", "row"), P("col", "row"))
    out_specs = (P("col", "row"), P("col", "row"), P("row", "col"))
    return jax.shard_map(shards, mesh=mesh, in_specs=in_specs, out_specs=out_specs, check_vma=False)
```

```python
import heapq

import jax
import jax.numpy as jnp
from jax import lax
from jax.experimental import pallas as pl
from jax.experimental.pallas import tpu as pltpu
from jax.sharding import PartitionSpec as P

MESH = pl.DeviceIdType.MESH
F32 = jnp.float32
BF16 = jnp.bfloat16

BLK = 128
NX, NZ, NH, NC, NCOL = 4, 12, 2, 2, 4
TOK = 8
PACK = 2 * TOK
HALF = 1024
ROWS = NH * NC * TOK
STEPS = NZ // 2
GROUPS = ((0, 1), (1, 3), (3, 5), (5, 7), (7, 9), (9, 11), (11, 12))
VMEM_LIMIT = 56 * 1024 * 1024
PIECES = 2
WAYS = (STEPS, STEPS - 1)

RING = (0, 1, 2, 3, 4, 5)
SKIP = (0, 0, 2, 2, 4, 4)
MIXED = (0, 1, 2, 2, 4, 4)

STREAMS = (
    (0, "zx", 256, 768, MIXED),
    (0, "xz", 0, 256, MIXED),
    (1, "zx", 256, 768, SKIP),
    (1, "xz", 0, 256, SKIP),
)
XCOUNT = [3 * len(GROUPS) if order == "zx" else 3 for _, order, _, _, _ in STREAMS]


def slots(g):
    return GROUPS[g]


def slot_offset(r):
    if r == 0:
        return 0
    if r == NZ - 1:
        return STEPS
    s = (r + 1) // 2
    return -s if r % 2 else s


def group_of(s):
    lo = 2 * s - 1
    g = next(g for g, (a, b) in enumerate(GROUPS) if a <= lo < b)
    return g, GROUPS[g][1] - GROUPS[g][0]


def make_plan(zlate=3.2, xlate=3.62, zrate=97e3, xrate=102e3, far_at=5.76, hidden_at=20.9, slack=1.2):
    rate = {"z": zrate, "x": xrate, "sib": 300e3}
    free = {"z": 0.0, "x": 0.0, "sib": 0.0}
    late = {"z": zlate, "x": xlate, "sib": 1.0 + slack}
    issue = 0.02
    ops, arrivals = [], []
    now = 0.0
    seen = {}
    ready = [0] * len(GROUPS)
    todo = []

    def start(msg, kind, size, hops=1):
        nonlocal now
        ops.append(("start", msg))
        now += issue
        free[kind] = max(free[kind], now) + size * hops / rate[kind]
        heapq.heappush(arrivals, (free[kind] + late[kind], msg))

    def size(i, slots_, xs):
        return slots_ * xs * PACK * STREAMS[i][3] * 2

    def nslots(g):
        lo, hi = slots(g)
        return hi - lo

    def send_z(i, s, ways=(0, 1)):
        for t in range(STEPS, 0, -1):
            for way in ways:
                if STREAMS[i][4][t - 1] == s and t <= WAYS[way]:
                    xs = 1 if STREAMS[i][1] == "zx" else NX
                    start(("z", i, way, t), "z", size(i, 1, xs), t - s)

    def send_x(i, g, k):
        start(("x", i, g, k), "x", size(i, nslots(g), 1))

    def send_sib(i, g, k):
        start(("sib", i, g, k), "sib", size(i, nslots(g), NX if k is None else 1))

    def begin(i):
        if STREAMS[i][1] == "zx":
            send_z(i, 0)
        send_x(i, 0, 0)
        send_x(i, 0, 2)
        if STREAMS[i][1] == "zx":
            send_sib(i, 0, 3)

    def count(key, full):
        seen[key] = seen.get(key, 0) + 1
        return seen[key] == full

    for i, stream in enumerate(STREAMS):
        if stream[0] == 0:
            begin(i)
    ops.append(("prepare",))
    now += 1.0
    heapq.heappush(arrivals, (far_at, ("far",)))
    heapq.heappush(arrivals, (hidden_at, ("hid",)))
    pieces = sum(4 if order == "zx" else 1 for _, order, _, _, _ in STREAMS)
    waiting = []
    while arrivals or todo:
        if todo and (not arrivals or arrivals[0][0] > now):
            todo.sort(key=lambda task: task[0] != "term")
            ops.append(todo.pop(0))
            now += 0.1 + 0.08 * nslots(ops[-1][1])
            continue
        at, msg = heapq.heappop(arrivals)
        now = max(now, at) + issue
        if msg[0] == "sib":
            g = msg[2]
            ready[g] += 1
            if ready[g] == pieces:
                todo.append(("term", g))
                (todo if seen.get("hid") else waiting).append(("wgrad", g))
            continue
        ops.append(("wait", msg))
        if msg[0] == "far":
            ops.extend(("start", ("hid", k)) for k in range(NCOL - 1))
            for i, stream in enumerate(STREAMS):
                if stream[0] == 1:
                    begin(i)
        elif msg[0] == "hid":
            seen["hid"] = 1
            todo += waiting
        elif msg[0] == "z":
            _, i, way, s = msg
            send_z(i, s, (way,))
            g, full = group_of(s)
            if count(("z", i, g), full):
                if STREAMS[i][1] == "zx":
                    send_x(i, g, 0)
                    send_x(i, g, 2)
                    send_sib(i, g, 3)
                else:
                    send_sib(i, g, None)
        else:
            _, i, g, k = msg
            if k == 0:
                send_x(i, g, 1)
            if STREAMS[i][1] == "zx":
                send_sib(i, g, k)
            elif count(("x", i, g), 3):
                send_z(i, 0)
                send_sib(i, g, None)
    return ops, now


def kernel(
    x_hbm, w_hbm, mask_hbm, gate_hbm, up_hbm,
    gg_hbm, gu_hbm, gd_hbm,
    xv, wv, mask, gv, uv, data, wm, hs, acc, tbuf, pbuf, rbuf, gg_ref, gu_ref, gd_ref,
    in_s, far_s, far_r, z_s, z_r, x_s, x_r, sib_s, sib_r, h_s, h_r, p_s, p_r, out_s,
):
    row, col = lax.axis_index("row"), lax.axis_index("col")
    c = lax.rem(row, NC)
    h = lax.rem(row // NC, NH)
    z0 = lax.rem(row // (NC * NH), NZ)
    x0 = row // (NC * NH * NZ)
    d = 1 - 2 * c
    xprev, xnext = lax.rem(x0 - d + NX, NX), lax.rem(x0 + d + NX, NX)

    def device(x, z, hh, cc):
        return (((x * NZ + z) * NH + hh) * NC + cc, col)

    xf = device(xnext, z0, h, c)
    xb = device(xprev, z0, h, c)
    zw = [[device(x0, lax.rem(z0 + t * e + NZ, NZ), h, c) for t in (1, 2)] for e in (d, -d)]
    sib = device(x0, z0, h, 1 - c)
    far = device(x0, z0, 1 - h, c)
    cols = [(row, lax.rem(col + k, NCOL)) for k in range(1, NCOL)]

    def copy(src, dst, send, recv, to):
        return pltpu.make_async_remote_copy(
            src_ref=src, dst_ref=dst, send_sem=send, recv_sem=recv,
            device_id=to, device_id_type=MESH,
        )

    barrier = pltpu.get_barrier_semaphore()
    peers = [xf, xb, *zw[0], *zw[1], sib, far] + cols
    loads = [
        pltpu.make_async_copy(src, dst, in_s.at[k])
        for k, (src, dst) in enumerate(
            ((x_hbm, xv), (w_hbm, wv), (mask_hbm, mask), (gate_hbm, gv), (up_hbm, uv))
        )
    ]
    loads[0].start()
    for peer in peers:
        pl.semaphore_signal(barrier, inc=1, device_id=peer, device_id_type=MESH)
    for load in loads[1:]:
        load.start()
    loads[0].wait()
    xs = xv[...].astype(F32)
    data[c, x0, 0, h] = jnp.concatenate([xs[:, :HALF], xs[:, HALF:]], axis=0).astype(BF16)
    pl.semaphore_wait(barrier, len(peers))

    def zslot(way, s):
        if s == 0:
            return 0
        if s == STEPS:
            return NZ - 1
        return 2 * s - 1 + c if way == 0 else 2 * s - c

    def cut(i, core, xsel, rsel):
        whose, _, lane, n, _ = STREAMS[i]
        return data.at[core, xsel, rsel, h if whose == 0 else 1 - h, :, pl.ds(lane, n)]

    def span(g):
        lo, hi = slots(g)
        return pl.ds(lo, hi - lo)

    xsem = [sum(XCOUNT[:i]) for i in range(len(STREAMS))]

    def describe(msg):
        kind = msg[0]
        if kind == "far":
            ref = data.at[c, x0, 0, h]
            return copy(ref, ref, far_s, far_r, far)
        if kind == "hid":
            ref = hs.at[col]
            return copy(ref, ref, h_s, h_r.at[msg[1]], cols[msg[1]])
        if kind == "part":
            _, g, k = msg
            src = pbuf.at[lax.rem(col + k + 1, NCOL), span(g)]
            return copy(src, rbuf.at[k, span(g)], p_s, p_r, cols[k])
        if kind == "z":
            _, i, way, s = msg
            xsel = x0 if STREAMS[i][1] == "zx" else slice(None)
            hops = s - STREAMS[i][4][s - 1]
            src, dst = cut(i, c, xsel, zslot(way, s - hops)), cut(i, c, xsel, zslot(way, s))
            return copy(src, dst, z_s.at[i], z_r.at[i, way * STEPS + s - 1], zw[way][hops - 1])
        if kind == "x":
            _, i, g, k = msg
            ref = cut(i, c, xprev if k == 1 else x0, span(g))
            return copy(ref, ref, x_s.at[i], x_r.at[xsem[i] + 3 * g + k], xb if k == 2 else xf)
        _, i, g, k = msg
        xsel = slice(None) if k is None else (xprev, lax.rem(x0 + 2, NX), xnext, x0)[k]
        ref = cut(i, c, xsel, span(g))
        return copy(ref, ref, sib_s, sib_r.at[g], sib)

    def blocks(g):
        lo, hi = slots(g)
        return [data[cc, :, lo:hi].reshape(NX * (hi - lo) * NH * PACK, HALF) for cc in range(NC)]

    def term(g):
        ref = data.at[1 - c, :, span(g)]
        copy(ref, ref, sib_s, sib_r.at[g], sib).wait_recv()
        lo, hi = slots(g)
        terms = []
        for block in blocks(g):
            t = lax.dot_general(
                block, wm[...], (((1,), (1,)), ((), ())), preferred_element_type=F32
            ).reshape(NX, hi - lo, NH, 2, TOK, 2 * BLK)
            terms.append(t[:, :, :, 0, :, :BLK] + t[:, :, :, 1, :, BLK:])
        value = jnp.concatenate(terms, axis=-2).reshape(NX, hi - lo, ROWS, BLK)
        tbuf[:, lo:hi] = value
        pbuf[:, lo:hi] = value.astype(BF16)
        for k in range(NCOL - 1):
            describe(("part", g, k)).start()

    started = []

    def wgrad(g):
        lo, hi = slots(g)
        hid = hs[:, lo:hi].astype(F32).reshape(NX, hi - lo, NH, NC, TOK, BLK)
        hids = []
        for cc in range(NC):
            v = hid[:, :, :, cc]
            zero = jnp.zeros_like(v)
            both = jnp.concatenate(
                [jnp.concatenate([v, zero], axis=-1), jnp.concatenate([zero, v], axis=-1)], axis=-2
            )
            hids.append(both.reshape(-1, 2 * BLK).astype(BF16))
        t = lax.dot_general(
            jnp.concatenate(hids, axis=0), jnp.concatenate(blocks(g), axis=0),
            (((0,), (0,)), ((), ())), preferred_element_type=F32,
        )
        acc[...] = acc[...] + t if started else t
        started.append(g)

    places = []
    for r in range(NZ):
        z = lax.rem(z0 + slot_offset(r) + NZ, NZ)
        places.append(pl.ds(pl.multiple_of(z * ROWS, ROWS), ROWS))

    def prepare():
        loads[3].wait()
        loads[4].wait()
        for r in range(NZ):
            gate = gv[places[r], :].astype(F32)
            up = uv[places[r], :].astype(F32)
            hs[col, r] = (gate * jax.nn.sigmoid(gate) * up).astype(BF16)
        loads[1].wait()
        loads[2].wait()
        for b in range(2 * HALF // BLK):
            part, at = divmod(b * BLK, HALF)
            scale = mask[0, b].astype(F32)
            value = wv[:, b * BLK:(b + 1) * BLK].astype(F32) * scale
            wm[part * BLK:(part + 1) * BLK, at:at + BLK] = value.astype(BF16)

    describe(("far",)).start()
    for op in make_plan()[0]:
        if op[0] == "prepare":
            prepare()
        elif op[0] == "term":
            term(op[1])
        elif op[0] == "wgrad":
            wgrad(op[1])
        elif op[0] == "start":
            describe(op[1]).start()
        elif op[1][0] == "hid":
            for k in range(NCOL - 1):
                describe(("hid", k)).wait_recv()
        else:
            describe(op[1]).wait_recv()

    for b in range(2 * HALF // BLK):
        part, at = divmod(b * BLK, HALF)
        scale = mask[0, b].astype(F32)
        value = acc[part * BLK:(part + 1) * BLK, at:at + BLK] * scale
        gd_ref[:, b * BLK:(b + 1) * BLK] = value.astype(BF16)
    outs = [
        pltpu.make_async_copy(src, dst, out_s.at[k])
        for k, (src, dst) in enumerate(((gg_ref, gg_hbm), (gu_ref, gu_hbm), (gd_ref, gd_hbm)))
    ]
    outs[2].start()
    copy(rbuf, rbuf, p_s, p_r, sib).wait_recv()
    for r in range(NZ):
        gate = gv[places[r], :].astype(F32)
        up = uv[places[r], :].astype(F32)
        sig = jax.nn.sigmoid(gate)
        gh = tbuf[col, r]
        for k in range(NCOL - 1):
            gh = gh + rbuf[k, r].astype(F32)
        gu_ref[places[r], :] = (gh * gate * sig).astype(BF16)
        gg_ref[places[r], :] = (gh * up * sig * (1.0 + gate * (1.0 - sig))).astype(BF16)

    outs[0].start()
    outs[1].start()
    describe(("far",)).wait_send()
    for i, (_, order, _, _, _) in enumerate(STREAMS):
        zref = cut(i, c, 0 if order == "zx" else slice(None), pl.ds(0, NZ - 1))
        copy(zref, zref, z_s.at[i], z_r.at[i, 0], sib).wait_send()
        xref = cut(i, c, pl.ds(0, 3), pl.ds(0, NZ) if order == "zx" else 0)
        copy(xref, xref, x_s.at[i], x_r.at[0], sib).wait_send()
    half = data.at[c]
    copy(half, half, sib_s, sib_r.at[0], sib).wait_send()
    three = hs.at[pl.ds(0, NCOL - 1)]
    copy(three, three, h_s, h_r.at[0], sib).wait_send()
    copy(rbuf, rbuf, p_s, p_r, sib).wait_send()
    for out in outs:
        out.wait()


def hand_over(*refs):
    sources, results, stages, sems = refs[:3], refs[3:6], refs[6:9], refs[9]
    loads, stores = [], []
    for src, dst, stage in zip(sources, results, stages):
        rows = src.shape[0] // PIECES
        for p in range(PIECES):
            at = pl.ds(p * rows, rows)
            n = len(loads)
            loads.append(pltpu.make_async_copy(src.at[at], stage.at[at], sems.at[n]))
            stores.append(pltpu.make_async_copy(stage.at[at], dst.at[at], sems.at[n]))
    for load in loads:
        load.start()
    for load, store in zip(loads, stores):
        load.wait()
        store.start()
    for store in stores:
        store.wait()


def shards(out_grad, down_weight, block_mask, gate_act, up_act):
    hbm = pl.BlockSpec(memory_space=pl.ANY)
    dma = pltpu.SemaphoreType.DMA
    units = down_weight.shape[0]
    n = len(STREAMS)
    xcount = sum(XCOUNT)
    scratch = [
        pltpu.VMEM(out_grad.shape, BF16),
        pltpu.VMEM(down_weight.shape, BF16),
        pltpu.SMEM(block_mask.shape, jnp.int32),
        pltpu.VMEM(gate_act.shape, BF16),
        pltpu.VMEM(up_act.shape, BF16),
        pltpu.VMEM((NC, NX, NZ, NH, PACK, HALF), BF16),
        pltpu.VMEM((2 * units, HALF), BF16),
        pltpu.VMEM((NX, NZ, ROWS, units), BF16),
        pltpu.VMEM((2 * units, HALF), F32),
        pltpu.VMEM((NX, NZ, ROWS, units), F32),
        pltpu.VMEM((NX, NZ, ROWS, units), BF16),
        pltpu.VMEM((NCOL - 1, NZ, ROWS, units), BF16),
        pltpu.VMEM(gate_act.shape, BF16),
        pltpu.VMEM(up_act.shape, BF16),
        pltpu.VMEM(down_weight.shape, BF16),
        dma((5,)), dma, dma, dma((n,)), dma((n, 2 * STEPS - 1)), dma((n,)), dma((xcount,)),
        dma, dma((len(GROUPS),)), dma, dma((NCOL - 1,)), dma, dma, dma((3,)),
    ]
    out_shape = (
        jax.ShapeDtypeStruct(gate_act.shape, BF16),
        jax.ShapeDtypeStruct(up_act.shape, BF16),
        jax.ShapeDtypeStruct(down_weight.shape, BF16),
    )
    results = pl.pallas_call(
        kernel,
        out_shape=out_shape,
        in_specs=[hbm] * 5,
        out_specs=(hbm,) * 3,
        scratch_shapes=scratch,
        compiler_params=pltpu.CompilerParams(
            collective_id=0, has_side_effects=True, vmem_limit_bytes=VMEM_LIMIT
        ),
    )(out_grad, down_weight, block_mask, gate_act, up_act)
    return pl.pallas_call(
        hand_over,
        out_shape=out_shape,
        in_specs=[hbm] * 3,
        out_specs=(hbm,) * 3,
        scratch_shapes=[pltpu.VMEM(o.shape, BF16) for o in out_shape] + [dma((3 * PIECES,))],
        compiler_params=pltpu.CompilerParams(vmem_limit_bytes=VMEM_LIMIT),
    )(*results)


def solution(mesh):
    in_specs = (P("row", "col"), P("row", "col"), P("row", "col"), P("col", "row"), P("col", "row"))
    out_specs = (P("col", "row"), P("col", "row"), P("row", "col"))
    return jax.shard_map(shards, mesh=mesh, in_specs=in_specs, out_specs=out_specs, check_vma=False)
```
